128 devices in a mesh: rep: 2 (over core), shard: 64 (over z, y, x).
Axes of the slice: x: 4, y: 4, z: 4, core: 2. Of those that a mesh axis runs over, the one named last changes fastest.
Arguments:
- gradients: bfloat16 [2, 81920, 1024], P('rep', 'shard')
- owner_table: int32 [80], replicated, may hold values from 0 to 63, as said below
- offsets: int32 [80], replicated, may hold values from 0 to 1264, as said below
- left_root: bfloat16 [128, 1024, 1024], P('shard')
- right_root: bfloat16 [128, 1024, 1024], P('shard', None, 'rep')
Outputs:
- graft_update: bfloat16 [81920, 1024], P('shard', 'rep')
- gram_left: float32 [128, 1024, 1024], P('shard', 'rep')
- gram_right: float32 [128, 1024, 1024], P('shard', 'rep')
The draws below stay inside these ranges and needn't reach their ends.
Inputs may be any that keep to these rules, and one draw needn't show every extreme that they name: `owner_table`: no owner holds more than 2 blocks, and some owner holds exactly 2. offsets are 16 times a permutation of 0 to 79.
All inputs are finite; a program needn't handle non-finite values.
Results may differ from the reference program's by a relative error of at most 0.0059.
Values may be sent and summed in bfloat16 or wider, within the bound.
No kernel may reach another device: no remote copies, remote signals or barrier semaphores. Data moves between devices by JAX's collectives and lax.ppermute only.
A program may use at most 128 MiB of HBM per device.

```python
import math
import jax
import jax.numpy as jnp
from jax import lax

BLOCK = 1024
BLOCKS = 80
SLOTS = 2
PIECE = 16
N_REP = 2
N_SHARD = 64


def draw_gradients(key, part):
    key = jax.random.fold_in(key, 5)
    keys = jax.random.split(key, 4)
    total_rows = N_SHARD * BLOCKS * PIECE
    column_ids = jnp.arange(BLOCK, dtype=jnp.float32)
    column_scale = jnp.exp(math.log(3.0) * column_ids / BLOCK) * jax.random.uniform(keys[0], (BLOCK,), jnp.float32, 1.0, 4.0) ** 1.0
    column_scale = jnp.exp(jnp.log(column_scale))
    row_scale = jnp.exp(jax.random.uniform(keys[1], (total_rows,), jnp.float32, 0.0, math.log(10.0)))
    noise = jax.random.normal(keys[3], (N_REP, total_rows, BLOCK), jnp.float32)
    values = 0.01 * noise * row_scale[None, :, None] * column_scale[None, None, :] / math.sqrt(N_REP)
    return values.astype(jnp.bfloat16)


def draw_owner_table(key, part):
    key = jax.random.fold_in(key, 11)
    keys = jax.random.split(key, 3)
    total = N_SHARD * SLOTS
    slot_ids = jnp.arange(total, dtype=jnp.int32)
    slot_owner = slot_ids // SLOTS
    busiest = jax.random.randint(keys[0], (), 0, N_SHARD)
    scores = jax.random.permutation(keys[1], total).astype(jnp.int32)
    scores = jnp.where(slot_owner == busiest, -1 - slot_ids % SLOTS, scores)
    ranked = jnp.argsort(scores, stable=True)
    owners = slot_owner[ranked[:BLOCKS]]
    return owners[jax.random.permutation(keys[2], BLOCKS)].astype(jnp.int32)


def draw_offsets(key, part):
    key = jax.random.fold_in(key, 12)
    return (PIECE * jax.random.permutation(key, BLOCKS)).astype(jnp.int32)


def root_matrices(key, count):
    keys = jax.random.split(key, 2)
    raw = jax.random.normal(keys[0], (count, BLOCK, BLOCK), jnp.float32)
    symmetric = 0.5 * (raw + jnp.swapaxes(raw, 1, 2))
    diagonal = jnp.exp(jax.random.uniform(keys[1], (count, BLOCK, 1), jnp.float32, math.log(0.5), math.log(2.0)))
    identity = jnp.eye(BLOCK, dtype=jnp.float32)[None]
    return 0.4 * symmetric / math.sqrt(BLOCK) + identity * diagonal


def draw_left_root(key, part):
    key = jax.random.fold_in(key, 21)
    return root_matrices(key, N_SHARD * SLOTS).astype(jnp.bfloat16)


def draw_right_root(key, part):
    key = jax.random.fold_in(key, 22)
    return root_matrices(key, N_SHARD * SLOTS).astype(jnp.bfloat16)


def setup_inputs(seed: int = 0) -> dict:
    splits = jax.random.split(jax.random.key(seed), 6)
    gradients = draw_gradients(jax.random.fold_in(splits[5], 71), 0)
    owner_table = draw_owner_table(jax.random.fold_in(splits[5], 71), 0)
    offsets = draw_offsets(jax.random.fold_in(splits[5], 71), 0)
    left_root = draw_left_root(jax.random.fold_in(splits[5], 71), 0)
    right_root = draw_right_root(jax.random.fold_in(splits[5], 71), 0)
    return dict(gradients=gradients, owner_table=owner_table, offsets=offsets, left_root=left_root, right_root=right_root)


EPSILON = 1e-06

def slot_targets(owner_table):
    block_ids = jnp.arange(owner_table.shape[0], dtype=jnp.int32)
    same_owner = owner_table[:, None] == owner_table[None, :]
    before = block_ids[:, None] < block_ids[None, :]
    slot_index = lax.optimization_barrier(jnp.sum(jnp.where(same_owner & before, 1, 0), axis=0)).astype(jnp.int32)
    return (owner_table * SLOTS + slot_index).astype(jnp.int32)

def reference(gradients, owner_table, offsets, left_root, right_root):
    summed = lax.optimization_barrier(jnp.sum(gradients.astype(jnp.float32), axis=0)).astype(jnp.bfloat16)
    flat_pieces = summed.reshape(N_SHARD, BLOCKS * PIECE, BLOCK)
    target = slot_targets(owner_table)
    entries = float(BLOCK * BLOCK)

    def per_block(index):
        rows_here = lax.dynamic_slice_in_dim(flat_pieces, offsets[index].astype(jnp.int32), PIECE, 1)
        grad_block = rows_here.reshape(BLOCK, BLOCK)
        left_gram = jnp.dot(grad_block, grad_block.T, preferred_element_type=jnp.float32)
        right_gram = jnp.dot(grad_block.T, grad_block, preferred_element_type=jnp.float32)
        half_done = jnp.dot(grad_block, right_root[target[index]], preferred_element_type=jnp.float32).astype(jnp.bfloat16)
        precond = jnp.dot(left_root[target[index]], half_done, preferred_element_type=jnp.float32)
        grad_sq = jnp.sum(jnp.square(grad_block.astype(jnp.float32)))
        pre_sq = jnp.sum(precond * precond)
        graft_scale = jnp.sqrt(grad_sq / entries / (pre_sq / entries + EPSILON))
        return (left_gram, right_gram, (precond * graft_scale).astype(jnp.bfloat16))
    lefts, rights, updates = lax.map(per_block, jnp.arange(BLOCKS, dtype=jnp.int32))
    gram_left = jnp.zeros((N_SHARD * SLOTS, BLOCK, BLOCK), jnp.float32).at[target].set(lefts)
    gram_right = jnp.zeros((N_SHARD * SLOTS, BLOCK, BLOCK), jnp.float32).at[target].set(rights)
    position = (offsets // PIECE).astype(jnp.int32)
    in_order = jnp.zeros((BLOCKS,), jnp.int32).at[position].set(jnp.arange(BLOCKS, dtype=jnp.int32))
    placed = updates[in_order].reshape(BLOCKS, N_SHARD, PIECE, BLOCK)
    placed = jnp.transpose(placed, (1, 0, 2, 3)).reshape(N_SHARD * BLOCKS * PIECE, BLOCK)
    return (placed, gram_left, gram_right)
```

```python
import functools

import jax
import jax.numpy as jnp
from jax import lax
from jax.experimental import pallas as pl
from jax.experimental.pallas import tpu as pltpu
from jax.sharding import PartitionSpec as P

EPSILON = 1e-06
VMEM_BYTES = 48 * 1024 * 1024
NT = (((1,), (1,)), ((), ()))
TN = (((0,), (0,)), ((), ()))
SWAP = [(0, 1), (1, 0)]


def cost(flops, nbytes):
    return pl.CostEstimate(flops=flops, bytes_accessed=nbytes, transcendentals=0)


def params():
    return pltpu.CompilerParams(vmem_limit_bytes=VMEM_BYTES)


def pack_kernel(slot, slots, piece, place_ref, rep_ref, mine_ref, theirs_ref, out_ref):
    def step(owner, carry):
        where = place_ref[owner * slots + slot]
        row = pl.multiple_of(jnp.maximum(where, 0) * piece, piece)
        total = mine_ref[pl.ds(row, piece), :].astype(jnp.float32) + theirs_ref[
            pl.ds(row, piece), :
        ].astype(jnp.float32)
        total = jnp.where(where >= 0, total, 0.0).astype(out_ref.dtype)
        out_ref[pl.ds(pl.multiple_of(owner * piece, piece), piece), :] = total
        return carry

    lax.fori_loop(0, out_ref.shape[0] // piece, step, 0, unroll=8)


def pack(slot, slots, piece, block, place, rep, mine, theirs):
    rows, strip = theirs.shape
    return pl.pallas_call(
        functools.partial(pack_kernel, slot, slots, piece),
        grid_spec=pltpu.PrefetchScalarGridSpec(
            num_scalar_prefetch=2,
            grid=(1,),
            in_specs=[
                pl.BlockSpec((rows, strip), lambda i, place, rep: (0, rep[0])),
                pl.BlockSpec((rows, strip), lambda i, place, rep: (0, 0)),
            ],
            out_specs=pl.BlockSpec((block, strip), lambda i, place, rep: (0, 0)),
        ),
        out_shape=jax.ShapeDtypeStruct((block, strip), theirs.dtype),
        compiler_params=params(),
        cost_estimate=cost(rows * strip, 2 * (2 * rows + block) * strip),
        name="pack",
    )(place, rep, mine, theirs)


def root_kernel(steps, rep_ref, own_ref, oth_ref, right_own, right_oth, left_ref, pre_ref, sums_ref, half):
    i = pl.program_id(0)
    tile = own_ref.shape[0]

    @pl.when(i == 0)
    def _():
        sums_ref[...] = jnp.zeros_like(sums_ref)

    @pl.when(i < steps)
    def _():
        own = own_ref[...]
        acc = jnp.dot(own, right_own[0], preferred_element_type=jnp.float32)
        acc += jnp.dot(oth_ref[...], right_oth[0], preferred_element_type=jnp.float32)
        half[pl.ds(pl.multiple_of(i * tile, tile), tile), :] = acc.astype(half.dtype)
        wide = own.astype(jnp.float32)
        sums_ref[0:1, :] += jnp.sum(wide * wide, axis=0, keepdims=True)

    @pl.when(i >= steps)
    def _():
        pre = jnp.dot(left_ref[0], half[...], preferred_element_type=jnp.float32)
        pre_ref[...] = pre
        sums_ref[1:2, :] += jnp.sum(pre * pre, axis=0, keepdims=True)


def apply_roots(slot, rep, own, oth, left_root, right_root):
    block, strip = own.shape
    steps = 2
    tile = block // steps
    return pl.pallas_call(
        functools.partial(root_kernel, steps),
        grid_spec=pltpu.PrefetchScalarGridSpec(
            num_scalar_prefetch=1,
            grid=(2 * steps,),
            in_specs=[
                pl.BlockSpec((tile, strip), lambda i, rep: (jnp.minimum(i, steps - 1), 0)),
                pl.BlockSpec((tile, strip), lambda i, rep: (jnp.minimum(i, steps - 1), 0)),
                pl.BlockSpec((1, strip, strip), lambda i, rep: (slot, rep[0], 0)),
                pl.BlockSpec((1, strip, strip), lambda i, rep: (slot, 1 - rep[0], 0)),
                pl.BlockSpec((1, tile, block), lambda i, rep: (slot, jnp.maximum(i - steps, 0), 0)),
            ],
            out_specs=[
                pl.BlockSpec((tile, strip), lambda i, rep: (jnp.maximum(i - steps, 0), 0)),
                pl.BlockSpec((8, strip), lambda i, rep: (0, 0)),
            ],
            scratch_shapes=[pltpu.VMEM((block, strip), jnp.bfloat16)],
        ),
        out_shape=[
            jax.ShapeDtypeStruct((block, strip), jnp.float32),
            jax.ShapeDtypeStruct((8, strip), jnp.float32),
        ],
        compiler_params=params(),
        cost_estimate=cost(4 * block * block * strip, 2 * block * (5 * strip + block)),
        name="roots",
    )(rep, own, oth, right_root, right_root, left_root)


def scale_kernel(entries, pre_ref, mine_ref, theirs_ref, out_ref):
    grad_sq = jnp.sum(mine_ref[0:1, :]) + jnp.sum(theirs_ref[0:1, :])
    pre_sq = jnp.sum(mine_ref[1:2, :]) + jnp.sum(theirs_ref[1:2, :])
    top = jnp.full((8, 128), grad_sq, jnp.float32) / entries
    bottom = jnp.full((8, 128), pre_sq, jnp.float32) / entries + EPSILON
    scale = jnp.sqrt(top / bottom)[0:1, 0:1]
    out_ref[...] = (pre_ref[...] * scale).astype(out_ref.dtype)


def apply_scale(pre, mine, theirs):
    block, strip = pre.shape
    steps = 4
    tile = block // steps
    return pl.pallas_call(
        functools.partial(scale_kernel, float(block * block)),
        grid=(steps,),
        in_specs=[
            pl.BlockSpec((tile, strip), lambda i: (i, 0)),
            pl.BlockSpec(mine.shape, lambda i: (0, 0)),
            pl.BlockSpec(mine.shape, lambda i: (0, 0)),
        ],
        out_specs=pl.BlockSpec((tile, strip), lambda i: (i, 0)),
        out_shape=jax.ShapeDtypeStruct((block, strip), jnp.bfloat16),
        compiler_params=params(),
        cost_estimate=cost(2 * block * strip, 6 * block * strip),
        name="graft",
    )(pre, mine, theirs)


def gram_kernel(steps, rep_ref, own_ref, oth_ref, *rest):
    left_out, right_out = rest[-2:]
    i = pl.program_id(0)
    rep = rep_ref[0]
    strip = own_ref.shape[1]
    tile = strip // steps
    row = pl.multiple_of(rep * strip + i * tile, tile)
    left = lax.dot_general(
        own_ref[pl.ds(row, tile), :], own_ref[...], NT, preferred_element_type=jnp.float32
    )
    left += lax.dot_general(
        oth_ref[pl.ds(row, tile), :], oth_ref[...], NT, preferred_element_type=jnp.float32
    )
    left_out[0] = left
    col = pl.multiple_of(i * tile, tile)
    mine = own_ref[:, pl.ds(col, tile)]
    here = pl.multiple_of(rep * strip, strip)
    there = pl.multiple_of((1 - rep) * strip, strip)
    right_out[0, :, pl.ds(here, strip)] = lax.dot_general(
        mine, own_ref[...], TN, preferred_element_type=jnp.float32
    )
    right_out[0, :, pl.ds(there, strip)] = lax.dot_general(
        mine, oth_ref[...], TN, preferred_element_type=jnp.float32
    )


def grams(slot, slots, rep, own, oth, previous):
    block, strip = own.shape
    steps = 2
    tile = strip // steps
    out = jax.ShapeDtypeStruct((slots, strip, block), jnp.float32)
    return pl.pallas_call(
        functools.partial(gram_kernel, steps),
        grid_spec=pltpu.PrefetchScalarGridSpec(
            num_scalar_prefetch=1,
            grid=(steps,),
            in_specs=[
                pl.BlockSpec((block, strip), lambda i, rep: (0, 0)),
                pl.BlockSpec((block, strip), lambda i, rep: (0, 0)),
            ]
            + [pl.BlockSpec(memory_space=pl.ANY)] * len(previous),
            out_specs=[pl.BlockSpec((1, tile, block), lambda i, rep: (slot, i, 0))] * 2,
        ),
        out_shape=[out, out],
        input_output_aliases={3 + k: k for k in range(len(previous))},
        compiler_params=params(),
        cost_estimate=cost(4 * block * block * strip, 4 * block * strip + 8 * block * strip),
        name="grams",
    )(rep, own, oth, *previous)


def place_kernel(slot, slots, piece, place_ref, blocks_ref, *rest):
    out_ref, sems = rest[-2:]
    count = blocks_ref.shape[0]

    def copy(owner):
        where = place_ref[owner * slots + slot]
        row = pl.multiple_of(jnp.maximum(where, 0) * piece, piece)
        return where, pltpu.make_async_copy(
            blocks_ref.at[owner], out_ref.at[pl.ds(row, piece), :], sems.at[owner]
        )

    def start(owner, carry):
        where, move = copy(owner)

        @pl.when(where >= 0)
        def _():
            move.start()

        return carry

    def finish(owner, carry):
        where, move = copy(owner)

        @pl.when(where >= 0)
        def _():
            move.wait()

        return carry

    lax.fori_loop(0, count, start, 0, unroll=4)
    lax.fori_loop(0, count, finish, 0, unroll=4)


def place_rows(slot, slots, rows, place, blocks, previous):
    count, piece, strip = blocks.shape
    return pl.pallas_call(
        functools.partial(place_kernel, slot, slots, piece),
        grid_spec=pltpu.PrefetchScalarGridSpec(
            num_scalar_prefetch=1,
            grid=(1,),
            in_specs=[pl.BlockSpec(memory_space=pl.ANY)] * (1 + len(previous)),
            out_specs=pl.BlockSpec(memory_space=pl.ANY),
            scratch_shapes=[pltpu.SemaphoreType.DMA((count,))],
        ),
        out_shape=jax.ShapeDtypeStruct((rows, strip), blocks.dtype),
        input_output_aliases={2 + k: k for k in range(len(previous))},
        compiler_params=params(),
        cost_estimate=cost(0, 4 * count * piece * strip),
        name="place",
    )(place, blocks, *previous)


def local(gradients, owner_table, offsets, left_root, right_root):
    shard_count = lax.axis_size("shard")
    slots, block = left_root.shape[:2]
    strip = right_root.shape[2]
    piece = block // shard_count
    rows = gradients.shape[1]
    block_ids = jnp.arange(offsets.shape[0], dtype=jnp.int32)
    me = lax.axis_index("rep").astype(jnp.int32)
    rep = me.reshape(1)

    mine = gradients[0]
    theirs = lax.ppermute(
        lax.dynamic_slice_in_dim(mine, (1 - me) * strip, strip, 1), "rep", SWAP
    )
    same_owner = owner_table[:, None] == owner_table[None, :]
    before = block_ids[:, None] < block_ids[None, :]
    rank = jnp.sum(jnp.where(same_owner & before, 1, 0), axis=0).astype(jnp.int32)
    target = owner_table * slots + rank
    slot_ids = jnp.arange(shard_count * slots, dtype=jnp.int32)
    holder = target[:, None] == slot_ids[None, :]
    place = jnp.sum(jnp.where(holder, (offsets // piece)[:, None] + 1, 0), axis=0) - 1
    place = place.astype(jnp.int32)

    def exchange(x):
        x = x.reshape(shard_count, piece, strip)
        return lax.all_to_all(x, "shard", split_axis=0, concat_axis=0, tiled=True)

    own = [
        exchange(pack(slot, slots, piece, block, place, rep, mine, theirs)).reshape(block, strip)
        for slot in range(slots)
    ]
    oth = [lax.ppermute(x, "rep", SWAP) for x in own]
    back = []
    for slot in range(slots):
        pre, sums = apply_roots(slot, rep, own[slot], oth[slot], left_root, right_root)
        other_sums = lax.ppermute(sums, "rep", SWAP)
        back.append(exchange(apply_scale(pre, sums, other_sums)))
    gram = ()
    update = ()
    for slot in range(slots):
        gram = tuple(grams(slot, slots, rep, own[slot], oth[slot], gram))
        update = (place_rows(slot, slots, rows, place, back[slot], update),)
    return (update[0], *gram)


def solution(mesh):
    in_specs = (P("rep", "shard", None), P(), P(), P("shard", None, None), P("shard", None, "rep"))
    out_specs = (P("shard", "rep"), P("shard", "rep", None), P("shard", "rep", None))
    return jax.shard_map(local, mesh=mesh, in_specs=in_specs, out_specs=out_specs, check_vma=False)
```

```python
import functools

import jax
import jax.numpy as jnp
from jax import lax
from jax.experimental import pallas as pl
from jax.experimental.pallas import tpu as pltpu
from jax.sharding import PartitionSpec as P

EPSILON = 1e-06
VMEM_BYTES = 48 * 1024 * 1024
NT = (((1,), (1,)), ((), ()))
TN = (((0,), (0,)), ((), ()))
SWAP = [(0, 1), (1, 0)]
BOTH = ("rep", "shard")


def cost(flops, nbytes):
    return pl.CostEstimate(flops=flops, bytes_accessed=nbytes, transcendentals=0)


def params():
    return pltpu.CompilerParams(vmem_limit_bytes=VMEM_BYTES)


def pack_kernel(place_ref, rep_ref, mine_ref, theirs_ref, out_ref):
    piece = out_ref.shape[1]
    base = pl.program_id(0) * out_ref.shape[0]

    def step(i, carry):
        where = place_ref[base + i]
        row = pl.multiple_of(jnp.maximum(where, 0) * piece, piece)
        total = mine_ref[pl.ds(row, piece), :].astype(jnp.float32) + theirs_ref[
            pl.ds(row, piece), :
        ].astype(jnp.float32)
        out_ref[i] = jnp.where(where >= 0, total, 0.0).astype(out_ref.dtype)
        return carry

    lax.fori_loop(0, out_ref.shape[0], step, 0, unroll=8)


def pack(pieces, piece, place, rep, mine, theirs):
    rows, strip = theirs.shape
    steps = 4
    return pl.pallas_call(
        pack_kernel,
        grid_spec=pltpu.PrefetchScalarGridSpec(
            num_scalar_prefetch=2,
            grid=(steps,),
            in_specs=[
                pl.BlockSpec((rows, strip), lambda i, place, rep: (0, rep[0])),
                pl.BlockSpec((rows, strip), lambda i, place, rep: (0, 0)),
            ],
            out_specs=pl.BlockSpec((pieces // steps, piece, strip), lambda i, place, rep: (i, 0, 0)),
        ),
        out_shape=jax.ShapeDtypeStruct((pieces, piece, strip), theirs.dtype),
        compiler_params=params(),
        cost_estimate=cost(rows * strip, 2 * (2 * rows + pieces * piece) * strip),
        name="pack",
    )(place, rep, mine, theirs)


def root_kernel(steps, rep_ref, grad_ref, right_own, right_oth, left_ref, out_ref, half, pre, sums):
    i = pl.program_id(0)
    rep = rep_ref[0]
    tile, strip = grad_ref.shape[1:]
    block = half.shape[1]

    @pl.when(i == 0)
    def _():
        sums[...] = jnp.zeros_like(sums)

    @pl.when(i < steps)
    def _():
        rows = pl.ds(pl.multiple_of(i * tile, tile), tile)
        first, second = grad_ref[0], grad_ref[1]
        for k, right in ((rep, right_own), (1 - rep, right_oth)):
            acc = jnp.dot(first, right[0, :strip, :], preferred_element_type=jnp.float32)
            acc += jnp.dot(second, right[0, strip:, :], preferred_element_type=jnp.float32)
            half[k, rows, :] = acc.astype(half.dtype)
        first, second = first.astype(jnp.float32), second.astype(jnp.float32)
        sums[0:1, :] += jnp.sum(first * first + second * second, axis=0, keepdims=True)

    @pl.when(i >= steps)
    def _():
        rows = pl.ds(pl.multiple_of((i - steps) * tile, tile), tile)
        for k in range(2):
            value = jnp.dot(left_ref[0], half[k], preferred_element_type=jnp.float32)
            pre[k, rows, :] = value
            sums[1:2, :] += jnp.sum(value * value, axis=0, keepdims=True)

    @pl.when(i == 2 * steps - 1)
    def _():
        entries = float(block * block)
        top = jnp.full((8, 128), jnp.sum(sums[0:1, :]), jnp.float32) / entries
        bottom = jnp.full((8, 128), jnp.sum(sums[1:2, :]), jnp.float32) / entries + EPSILON
        scale = jnp.sqrt(top / bottom)[0:1, 0:1]
        for k in range(2):
            out_ref[k] = (pre[k] * scale).astype(out_ref.dtype)


def apply_roots(rep, grad, left_root, right_root, right_other):
    strips, block, strip = grad.shape
    steps = 2
    tile = block // steps
    return pl.pallas_call(
        functools.partial(root_kernel, steps),
        grid_spec=pltpu.PrefetchScalarGridSpec(
            num_scalar_prefetch=1,
            grid=(2 * steps,),
            in_specs=[
                pl.BlockSpec((strips, tile, strip), lambda i, rep: (0, jnp.minimum(i, steps - 1), 0)),
                pl.BlockSpec((1, block, strip), lambda i, rep: (rep[0], 0, 0)),
                pl.BlockSpec((1, block, strip), lambda i, rep: (0, 0, 0)),
                pl.BlockSpec(
                    (1, tile, block), lambda i, rep: (rep[0], jnp.maximum(i - steps, 0), 0)
                ),
            ],
            out_specs=pl.BlockSpec(grad.shape, lambda i, rep: (0, 0, 0)),
            scratch_shapes=[
                pltpu.VMEM(grad.shape, jnp.bfloat16),
                pltpu.VMEM(grad.shape, jnp.float32),
                pltpu.VMEM((8, strip), jnp.float32),
            ],
        ),
        out_shape=jax.ShapeDtypeStruct(grad.shape, jnp.bfloat16),
        compiler_params=params(),
        cost_estimate=cost(4 * block**3, 8 * block * block),
        name="roots",
    )(rep, grad, right_root, right_other, left_root)


def gram_kernel(steps, rep_ref, own_ref, oth_ref, left_out, right_out):
    i = pl.program_id(0)
    rep = rep_ref[0]

    def form(grad_ref):
        strips, _, strip = grad_ref.shape
        tile = strip // steps
        begin = pl.multiple_of((i % steps) * tile, tile)
        rows = pl.ds(pl.multiple_of(rep * strip + begin, tile), tile)
        left = lax.dot_general(
            grad_ref[0, rows, :], grad_ref[0], NT, preferred_element_type=jnp.float32
        )
        for k in range(1, strips):
            left += lax.dot_general(
                grad_ref[k, rows, :], grad_ref[k], NT, preferred_element_type=jnp.float32
            )
        left_out[0] = left
        columns = grad_ref[rep, :, pl.ds(begin, tile)]
        for k in range(strips):
            right_out[0, :, k * strip : (k + 1) * strip] = lax.dot_general(
                columns, grad_ref[k], TN, preferred_element_type=jnp.float32
            )

    pl.when(i < steps)(lambda: form(own_ref))
    pl.when(i >= steps)(lambda: form(oth_ref))


def grams(rep, own, oth):
    slots, block, strip = own.shape
    steps = 2
    tile = strip // steps
    out = jax.ShapeDtypeStruct((slots, strip, block), jnp.float32)

    def where(i, rep):
        return (jnp.where(i < steps, rep[0], 1 - rep[0]), i % steps, 0)

    return pl.pallas_call(
        functools.partial(gram_kernel, steps),
        grid_spec=pltpu.PrefetchScalarGridSpec(
            num_scalar_prefetch=1,
            grid=(2 * steps,),
            in_specs=[pl.BlockSpec(own.shape, lambda i, rep: (0, 0, 0))] * 2,
            out_specs=[pl.BlockSpec((1, tile, block), where)] * 2,
        ),
        out_shape=[out, out],
        compiler_params=params(),
        cost_estimate=cost(8 * block * block * strip, 24 * block * strip),
        name="grams",
    )(rep, own, oth)


def place_kernel(source_ref, row_ref, pieces_ref, out_ref, sem):
    piece = pieces_ref.shape[1]

    def start(b, carry):
        row = pl.multiple_of(row_ref[b], piece)
        pltpu.make_async_copy(
            pieces_ref.at[source_ref[b]], out_ref.at[pl.ds(row, piece), :], sem
        ).start()
        return carry

    lax.fori_loop(0, row_ref.shape[0], start, 0, unroll=4)
    pltpu.make_async_copy(out_ref, out_ref, sem).wait()


def place_rows(rows, source, row, pieces):
    _, piece, strip = pieces.shape
    return pl.pallas_call(
        place_kernel,
        grid_spec=pltpu.PrefetchScalarGridSpec(
            num_scalar_prefetch=2,
            grid=(1,),
            in_specs=[pl.BlockSpec(memory_space=pl.ANY)],
            out_specs=pl.BlockSpec(memory_space=pl.ANY),
            scratch_shapes=[pltpu.SemaphoreType.DMA],
        ),
        out_shape=jax.ShapeDtypeStruct((rows, strip), pieces.dtype),
        compiler_params=params(),
        cost_estimate=cost(0, 4 * rows * strip),
        name="place",
    )(source, row, pieces)


def local(gradients, owner_table, offsets, left_root, right_root):
    shard_count = lax.axis_size("shard")
    slots, block = left_root.shape[:2]
    strip = right_root.shape[2]
    piece = block // shard_count
    rows = gradients.shape[1]
    block_ids = jnp.arange(offsets.shape[0], dtype=jnp.int32)
    me = lax.axis_index("rep").astype(jnp.int32)
    rep = me.reshape(1)

    mine = gradients[0]
    theirs = lax.ppermute(
        lax.dynamic_slice_in_dim(mine, (1 - me) * strip, strip, 1), "rep", SWAP
    )
    same_owner = owner_table[:, None] == owner_table[None, :]
    before = block_ids[:, None] < block_ids[None, :]
    rank = jnp.sum(jnp.where(same_owner & before, 1, 0), axis=0).astype(jnp.int32)
    holder_id = rank * shard_count + owner_table
    holder_ids = jnp.arange(slots * shard_count, dtype=jnp.int32)
    held = holder_id[:, None] == holder_ids[None, :]
    place = jnp.sum(jnp.where(held, (offsets // piece)[:, None] + 1, 0), axis=0) - 1
    place = place.astype(jnp.int32)

    def exchange(x):
        return lax.all_to_all(x, BOTH, split_axis=0, concat_axis=0, tiled=True)

    packed = pack(slots * shard_count, piece, place, rep, mine, theirs)
    packed, right_root = lax.optimization_barrier((packed, right_root))
    right_other = lax.ppermute(
        lax.dynamic_slice_in_dim(right_root, 1 - me, 1, 0), "rep", SWAP
    )
    grad = exchange(packed).reshape(slots, block, strip)
    update = apply_roots(rep, grad, left_root, right_root, right_other)
    update, grad = lax.optimization_barrier((update, grad))
    back = exchange(update.reshape(packed.shape))
    grad_other = lax.ppermute(grad, "rep", SWAP)
    gram_left, gram_right = grams(rep, grad, grad_other)
    holder_id, gram_left = lax.optimization_barrier((holder_id, gram_left))
    return place_rows(rows, holder_id, offsets, back), gram_left, gram_right


def solution(mesh):
    in_specs = (P("rep", "shard", None), P(), P(), P("shard", None, None), P("shard", None, "rep"))
    out_specs = (P("shard", "rep"), P("shard", "rep", None), P("shard", "rep", None))
    return jax.shard_map(local, mesh=mesh, in_specs=in_specs, out_specs=out_specs, check_vma=False)
```

```python
import functools

import jax
import jax.numpy as jnp
from jax import lax
from jax.experimental import pallas as pl
from jax.experimental.pallas import tpu as pltpu
from jax.sharding import PartitionSpec as P

EPSILON = 1e-06
VMEM_BYTES = 24 * 1024 * 1024
NT = (((1,), (1,)), ((), ()))
TN = (((0,), (0,)), ((), ()))
SWAP = [(0, 1), (1, 0)]
BOTH = ("rep", "shard")


def cost(flops, nbytes):
    return pl.CostEstimate(flops=flops, bytes_accessed=nbytes, transcendentals=0)


def params():
    return pltpu.CompilerParams(vmem_limit_bytes=VMEM_BYTES)


def in_vmem(x):
    return pltpu.with_memory_space_constraint(x, pltpu.VMEM)


def in_hbm(x):
    return pltpu.with_memory_space_constraint(x, pltpu.HBM)


def strip_kernel(steps, which_ref, rows_ref, strip_ref, sems):
    rows, strip = strip_ref.shape
    columns = pl.ds(pl.multiple_of(which_ref[0] * strip, strip), strip)
    moves = []
    for k in range(steps):
        here = pl.ds(k * (rows // steps), rows // steps)
        move = pltpu.make_async_copy(rows_ref.at[here, columns], strip_ref.at[here], sems.at[k])
        move.start()
        moves.append(move)
    for move in moves:
        move.wait()


def take_strip(strip, which, gradients):
    rows = gradients.shape[0]
    steps = 4
    return pl.pallas_call(
        functools.partial(strip_kernel, steps),
        grid_spec=pltpu.PrefetchScalarGridSpec(
            num_scalar_prefetch=1,
            grid=(1,),
            in_specs=[pl.BlockSpec(memory_space=pltpu.HBM)],
            out_specs=pl.BlockSpec(memory_space=pltpu.VMEM),
            scratch_shapes=[pltpu.SemaphoreType.DMA((steps,))],
        ),
        out_shape=pltpu.VMEM((rows, strip), gradients.dtype),
        compiler_params=params(),
        cost_estimate=cost(0, 4 * rows * strip),
        name="strip",
    )(which, in_hbm(gradients))


def fetch_kernel(which_ref, left_ref, left_out, sems):
    moves = []
    for k in range(4):
        rows = pl.ds(k * (left_out.shape[0] // 4), left_out.shape[0] // 4)
        move = pltpu.make_async_copy(
            left_ref.at[which_ref[0], rows], left_out.at[rows], sems.at[k]
        )
        move.start()
        moves.append(move)
    for move in moves:
        move.wait()


def fetch_root(which, left_root):
    return pl.pallas_call(
        fetch_kernel,
        grid_spec=pltpu.PrefetchScalarGridSpec(
            num_scalar_prefetch=1,
            grid=(1,),
            in_specs=[pl.BlockSpec(memory_space=pltpu.HBM)],
            out_specs=pl.BlockSpec(memory_space=pltpu.VMEM),
            scratch_shapes=[pltpu.SemaphoreType.DMA((4,))],
        ),
        out_shape=pltpu.VMEM(left_root.shape[1:], left_root.dtype),
        compiler_params=params(),
        cost_estimate=cost(0, 4 * left_root[0].size),
        name="fetch",
    )(which, in_hbm(left_root))


def pack_kernel(steps, place_ref, mine_ref, theirs_ref, out_ref, total, sems):
    pieces, piece, _ = total.shape
    chunk = pieces // steps
    moves = []
    for k in range(steps):

        def step(i, carry, k=k):
            where = place_ref[k * chunk + i]
            rows = pl.ds(pl.multiple_of(jnp.maximum(where, 0) * piece, piece), piece)
            both = mine_ref[rows, :] + theirs_ref[rows, :]
            total[k * chunk + i] = jnp.where(where >= 0, both, jnp.zeros_like(both))
            return carry

        lax.fori_loop(0, chunk, step, 0, unroll=8)
        here = pl.ds(k * chunk, chunk)
        move = pltpu.make_async_copy(total.at[here], out_ref.at[here], sems.at[k])
        move.start()
        moves.append(move)
    for move in moves:
        move.wait()


def pack(pieces, piece, place, mine, theirs):
    rows, strip = theirs.shape
    steps = 8
    return pl.pallas_call(
        functools.partial(pack_kernel, steps),
        grid_spec=pltpu.PrefetchScalarGridSpec(
            num_scalar_prefetch=1,
            grid=(1,),
            in_specs=[pl.BlockSpec(memory_space=pltpu.VMEM)] * 2,
            out_specs=pl.BlockSpec(memory_space=pltpu.HBM),
            scratch_shapes=[
                pltpu.VMEM((pieces, piece, strip), theirs.dtype),
                pltpu.SemaphoreType.DMA((steps,)),
            ],
        ),
        out_shape=pltpu.HBM((pieces, piece, strip), theirs.dtype),
        compiler_params=params(),
        cost_estimate=cost(rows * strip, 2 * pieces * piece * strip),
        name="pack",
    )(place, in_vmem(mine), in_vmem(theirs))


def root_kernel(
    tiles,
    steps,
    rep_ref,
    grad_ref,
    right_ref,
    right_oth,
    left_ref,
    out_ref,
    kept_ref,
    grad,
    right_own,
    half,
    pre,
    ready,
    sems,
    own_sem,
    kept_sem,
):
    rep = rep_ref[0]
    strips, block, strip = grad.shape
    arrivals = []
    for i in range(tiles):
        rows = pl.ds(i * (block // tiles), block // tiles)
        for k in range(strips):
            move = pltpu.make_async_copy(
                grad_ref.at[k, rows], grad.at[k, rows], sems.at[len(arrivals)]
            )
            move.start()
            arrivals.append(move)
        if i == 0:
            own = pltpu.make_async_copy(right_ref.at[rep], right_own, own_sem)
            own.start()
    grad_sq = jnp.zeros((1, strip), jnp.float32)
    for i in range(tiles):
        rows = pl.ds(i * (block // tiles), block // tiles)
        for k in range(strips):
            arrivals[strips * i + k].wait()
        wide = jnp.concatenate([grad[k, rows, :] for k in range(strips)], axis=1)
        for k, right in ((1, right_oth.at[0]), (0, right_own)):
            if i == 0 and k == 0:
                own.wait()
            acc = jnp.dot(wide, right[...], preferred_element_type=jnp.float32)
            half[k, rows, :] = acc.astype(half.dtype)
        for k in range(strips):
            value = grad[k, rows, :].astype(jnp.float32)
            grad_sq += jnp.sum(value * value, axis=0, keepdims=True)
    keep = pltpu.make_async_copy(grad, kept_ref, kept_sem)
    keep.start()
    pre_sq = jnp.zeros((1, strip), jnp.float32)
    for k in range(strips):
        value = jnp.dot(left_ref[...], half[k], preferred_element_type=jnp.float32)
        pre[k] = value
        pre_sq += jnp.sum(value * value, axis=0, keepdims=True)
    entries = float(block * block)
    top = jnp.full((8, 128), jnp.sum(grad_sq), jnp.float32) / entries
    bottom = jnp.full((8, 128), jnp.sum(pre_sq), jnp.float32) / entries + EPSILON
    scale = jnp.sqrt(top / bottom)[0:1, 0:1]
    moves = [keep]
    for k, c in ((0, rep), (1, 1 - rep)):
        for j in range(steps):
            rows = pl.ds(j * (block // steps), block // steps)
            ready[k, rows, :] = (pre[k, rows, :] * scale).astype(ready.dtype)
            move = pltpu.make_async_copy(
                ready.at[k, rows], out_ref.at[c, rows], sems.at[strips * tiles + len(moves) - 1]
            )
            move.start()
            moves.append(move)
    for move in moves:
        move.wait()


def apply_roots(rep, grad, left, right_root, right_oth):
    strips, block, strip = grad.shape
    tiles = 2
    steps = 4
    out = pltpu.HBM(grad.shape, jnp.bfloat16)
    return pl.pallas_call(
        functools.partial(root_kernel, tiles, steps),
        grid_spec=pltpu.PrefetchScalarGridSpec(
            num_scalar_prefetch=1,
            grid=(1,),
            in_specs=[
                pl.BlockSpec(memory_space=pl.ANY),
                pl.BlockSpec(memory_space=pltpu.HBM),
                pl.BlockSpec(memory_space=pltpu.VMEM),
                pl.BlockSpec(memory_space=pltpu.VMEM),
            ],
            out_specs=[pl.BlockSpec(memory_space=pltpu.HBM)] * 2,
            scratch_shapes=[
                pltpu.VMEM(grad.shape, jnp.bfloat16),
                pltpu.VMEM((block, strip), jnp.bfloat16),
                pltpu.VMEM(grad.shape, jnp.bfloat16),
                pltpu.VMEM(grad.shape, jnp.float32),
                pltpu.VMEM(grad.shape, jnp.bfloat16),
                pltpu.SemaphoreType.DMA((strips * (steps + tiles),)),
                pltpu.SemaphoreType.DMA,
                pltpu.SemaphoreType.DMA,
            ],
        ),
        out_shape=[out, out],
        compiler_params=params(),
        cost_estimate=cost(4 * block**3, 4 * block * block),
        name="roots",
    )(rep, grad, in_hbm(right_root), in_vmem(right_oth), in_vmem(left))


def gram_kernel(steps, rep_ref, own_ref, oth_ref, left_out, right_out):
    i = pl.program_id(0)
    rep = rep_ref[0]

    def form(grad_ref):
        strips, _, strip = grad_ref.shape
        tile = strip // steps
        begin = pl.multiple_of((i % steps) * tile, tile)
        rows = pl.ds(pl.multiple_of(rep * strip + begin, tile), tile)
        left = lax.dot_general(
            grad_ref[0, rows, :], grad_ref[0], NT, preferred_element_type=jnp.float32
        )
        for k in range(1, strips):
            left += lax.dot_general(
                grad_ref[k, rows, :], grad_ref[k], NT, preferred_element_type=jnp.float32
            )
        left_out[0] = left
        columns = grad_ref[rep, :, pl.ds(begin, tile)]
        for k in range(strips):
            right_out[0, :, k * strip : (k + 1) * strip] = lax.dot_general(
                columns, grad_ref[k], TN, preferred_element_type=jnp.float32
            )

    pl.when(i < steps)(lambda: form(own_ref))
    pl.when(i >= steps)(lambda: form(oth_ref))


def grams(rep, own, oth):
    slots, block, strip = own.shape
    steps = 2
    tile = strip // steps
    out = jax.ShapeDtypeStruct((slots, strip, block), jnp.float32)

    def where(i, rep):
        return (jnp.where(i < steps, rep[0], 1 - rep[0]), i % steps, 0)

    return pl.pallas_call(
        functools.partial(gram_kernel, steps),
        grid_spec=pltpu.PrefetchScalarGridSpec(
            num_scalar_prefetch=1,
            grid=(2 * steps,),
            in_specs=[pl.BlockSpec(own.shape, lambda i, rep: (0, 0, 0))] * 2,
            out_specs=[pl.BlockSpec((1, tile, block), where)] * 2,
        ),
        out_shape=[out, out],
        compiler_params=params(),
        cost_estimate=cost(8 * block * block * strip, 24 * block * strip),
        name="grams",
    )(rep, own, oth)


def place_kernel(source_ref, row_ref, pieces_ref, out_ref, sem):
    piece = pieces_ref.shape[1]

    def start(b, carry):
        row = pl.multiple_of(row_ref[b], piece)
        pltpu.make_async_copy(
            pieces_ref.at[source_ref[b]], out_ref.at[pl.ds(row, piece), :], sem
        ).start()
        return carry

    lax.fori_loop(0, row_ref.shape[0], start, 0, unroll=4)
    pltpu.make_async_copy(out_ref, out_ref, sem).wait()


def place_rows(rows, source, row, pieces):
    _, piece, strip = pieces.shape
    return pl.pallas_call(
        place_kernel,
        grid_spec=pltpu.PrefetchScalarGridSpec(
            num_scalar_prefetch=2,
            grid=(1,),
            in_specs=[pl.BlockSpec(memory_space=pl.ANY)],
            out_specs=pl.BlockSpec(memory_space=pl.ANY),
            scratch_shapes=[pltpu.SemaphoreType.DMA],
        ),
        out_shape=jax.ShapeDtypeStruct((rows, strip), pieces.dtype),
        compiler_params=params(),
        cost_estimate=cost(0, 4 * rows * strip),
        name="place",
    )(source, row, pieces)


def local(gradients, owner_table, offsets, left_root, right_root):
    shard_count = lax.axis_size("shard")
    slots, block = left_root.shape[:2]
    strip = right_root.shape[2]
    piece = block // shard_count
    rows = gradients.shape[1]
    block_ids = jnp.arange(offsets.shape[0], dtype=jnp.int32)
    me = lax.axis_index("rep").astype(jnp.int32)
    rep = me.reshape(1)

    send = take_strip(strip, 1 - rep, gradients[0])
    theirs = lax.ppermute(send, "rep", SWAP)
    send, whole = lax.optimization_barrier((send, gradients[0]))
    mine = take_strip(strip, rep, whole)
    same_owner = owner_table[:, None] == owner_table[None, :]
    before = block_ids[:, None] < block_ids[None, :]
    rank = jnp.sum(jnp.where(same_owner & before, 1, 0), axis=0).astype(jnp.int32)
    holder_id = rank * shard_count + owner_table
    holder_ids = jnp.arange(slots * shard_count, dtype=jnp.int32)
    held = holder_id[:, None] == holder_ids[None, :]
    place = jnp.sum(jnp.where(held, (offsets // piece)[:, None] + 1, 0), axis=0) - 1
    place = place.astype(jnp.int32)

    def exchange(x):
        return lax.all_to_all(x, BOTH, split_axis=0, concat_axis=0, tiled=True)

    packed = pack(slots * shard_count, piece, place, mine, theirs)
    packed, left_root, right_root = lax.optimization_barrier((packed, left_root, right_root))
    right_oth = lax.ppermute(
        lax.dynamic_slice_in_dim(right_root, 1 - me, 1, 0), "rep", SWAP
    )
    left = fetch_root(rep, left_root)
    grad = exchange(packed).reshape(slots, block, strip)
    update, grad = apply_roots(rep, grad, left, right_root, right_oth)
    update, grad = lax.optimization_barrier((update, grad))
    back = exchange(update.reshape(packed.shape))
    grad_other = lax.ppermute(grad, "rep", SWAP)
    gram_left, gram_right = grams(rep, grad, grad_other)
    holder_id, gram_left = lax.optimization_barrier((holder_id, gram_left))
    return place_rows(rows, holder_id, offsets, back), gram_left, gram_right


def solution(mesh):
    in_specs = (P("rep", "shard", None), P(), P(), P("shard", None, None), P("shard", None, "rep"))
    out_specs = (P("shard", "rep"), P("shard", "rep", None), P("shard", "rep", None))
    return jax.shard_map(local, mesh=mesh, in_specs=in_specs, out_specs=out_specs, check_vma=False)
```

```python
import functools

import jax
import jax.numpy as jnp
from jax import lax
from jax.experimental import pallas as pl
from jax.experimental.pallas import tpu as pltpu
from jax.sharding import PartitionSpec as P

EPSILON = 1e-06
VMEM_BYTES = 24 * 1024 * 1024
NT = (((1,), (1,)), ((), ()))
TN = (((0,), (0,)), ((), ()))
SWAP = [(0, 1), (1, 0)]
BOTH = ("rep", "shard")


def cost(flops, nbytes):
    return pl.CostEstimate(flops=flops, bytes_accessed=nbytes, transcendentals=0)


def params():
    return pltpu.CompilerParams(vmem_limit_bytes=VMEM_BYTES)


def in_vmem(x):
    return pltpu.with_memory_space_constraint(x, pltpu.VMEM)


def in_hbm(x):
    return pltpu.with_memory_space_constraint(x, pltpu.HBM)


def strip_kernel(steps, which_ref, rows_ref, strip_ref, sems):
    rows, strip = strip_ref.shape
    columns = pl.ds(pl.multiple_of(which_ref[0] * strip, strip), strip)
    moves = []
    for k in range(steps):
        here = pl.ds(k * (rows // steps), rows // steps)
        move = pltpu.make_async_copy(rows_ref.at[here, columns], strip_ref.at[here], sems.at[k])
        move.start()
        moves.append(move)
    for move in moves:
        move.wait()


def take_strip(strip, which, gradients):
    rows = gradients.shape[0]
    steps = 4
    return pl.pallas_call(
        functools.partial(strip_kernel, steps),
        grid_spec=pltpu.PrefetchScalarGridSpec(
            num_scalar_prefetch=1,
            grid=(1,),
            in_specs=[pl.BlockSpec(memory_space=pltpu.HBM)],
            out_specs=pl.BlockSpec(memory_space=pltpu.VMEM),
            scratch_shapes=[pltpu.SemaphoreType.DMA((steps,))],
        ),
        out_shape=pltpu.VMEM((rows, strip), gradients.dtype),
        compiler_params=params(),
        cost_estimate=cost(0, 4 * rows * strip),
        name="strip",
    )(which, in_hbm(gradients))


def fetch_kernel(right_ref, right_out, sems):
    moves = []
    for k in range(sems.shape[0]):
        count = right_out.shape[0] // sems.shape[0]
        rows = pl.ds(k * count, count)
        move = pltpu.make_async_copy(right_ref.at[0, rows], right_out.at[rows], sems.at[k])
        move.start()
        moves.append(move)
    for move in moves:
        move.wait()


def fetch(right):
    return pl.pallas_call(
        fetch_kernel,
        in_specs=[pl.BlockSpec(memory_space=pltpu.HBM)],
        out_specs=pl.BlockSpec(memory_space=pltpu.VMEM),
        scratch_shapes=[pltpu.SemaphoreType.DMA((2,))],
        out_shape=pltpu.VMEM(right.shape[1:], right.dtype),
        compiler_params=params(),
        cost_estimate=cost(0, 4 * right.size),
        name="fetch",
    )(in_hbm(right))


def pack_kernel(steps, place_ref, mine_ref, theirs_ref, out_ref, total, sems):
    pieces, piece, _ = total.shape
    chunk = pieces // steps
    moves = []
    for k in range(steps):

        def step(i, carry, k=k):
            where = place_ref[k * chunk + i]
            rows = pl.ds(pl.multiple_of(jnp.maximum(where, 0) * piece, piece), piece)
            both = mine_ref[rows, :] + theirs_ref[rows, :]
            total[k * chunk + i] = jnp.where(where >= 0, both, jnp.zeros_like(both))
            return carry

        lax.fori_loop(0, chunk, step, 0, unroll=8)
        here = pl.ds(k * chunk, chunk)
        move = pltpu.make_async_copy(total.at[here], out_ref.at[here], sems.at[k])
        move.start()
        moves.append(move)
    for move in moves:
        move.wait()


def pack(pieces, piece, place, mine, theirs):
    rows, strip = theirs.shape
    steps = 8
    return pl.pallas_call(
        functools.partial(pack_kernel, steps),
        grid_spec=pltpu.PrefetchScalarGridSpec(
            num_scalar_prefetch=1,
            grid=(1,),
            in_specs=[pl.BlockSpec(memory_space=pltpu.VMEM)] * 2,
            out_specs=pl.BlockSpec(memory_space=pltpu.HBM),
            scratch_shapes=[
                pltpu.VMEM((pieces, piece, strip), theirs.dtype),
                pltpu.SemaphoreType.DMA((steps,)),
            ],
        ),
        out_shape=pltpu.HBM((pieces, piece, strip), theirs.dtype),
        compiler_params=params(),
        cost_estimate=cost(rows * strip, 2 * pieces * piece * strip),
        name="pack",
    )(place, in_vmem(mine), in_vmem(theirs))


def root_kernel(
    steps,
    rep_ref,
    grad_ref,
    right_ref,
    right_oth,
    left_ref,
    out_ref,
    kept_ref,
    right_own,
    left,
    half,
    pre,
    ready,
    sems,
    in_sems,
    kept_sem,
):
    rep = rep_ref[0]
    strips, block, strip = half.shape
    fetch_right = pltpu.make_async_copy(right_ref.at[rep], right_own, in_sems.at[0])
    fetch_left = pltpu.make_async_copy(left_ref.at[rep], left, in_sems.at[1])
    keep = pltpu.make_async_copy(grad_ref, kept_ref, kept_sem)
    fetch_right.start()
    fetch_left.start()
    for k, right in ((1, right_oth), (0, right_own)):
        if k == 0:
            fetch_right.wait()
        wide = jnp.concatenate([grad_ref[j] for j in range(strips)], axis=1)
        acc = jnp.dot(wide, right[...], preferred_element_type=jnp.float32)
        half[k] = acc.astype(half.dtype)
    grad_sq = jnp.zeros((1, strip), jnp.float32)
    for k in range(strips):
        value = grad_ref[k].astype(jnp.float32)
        grad_sq += jnp.sum(value * value, axis=0, keepdims=True)
    fetch_left.wait()
    keep.start()
    pre_sq = jnp.zeros((1, strip), jnp.float32)
    for k in range(strips):
        value = jnp.dot(left[...], half[k], preferred_element_type=jnp.float32)
        pre[k] = value
        pre_sq += jnp.sum(value * value, axis=0, keepdims=True)
    entries = float(block * block)
    top = jnp.full((8, 128), jnp.sum(grad_sq), jnp.float32) / entries
    bottom = jnp.full((8, 128), jnp.sum(pre_sq), jnp.float32) / entries + EPSILON
    scale = jnp.sqrt(top / bottom)[0:1, 0:1]
    moves = [keep]
    for k, c in ((0, rep), (1, 1 - rep)):
        for j in range(steps):
            rows = pl.ds(j * (block // steps), block // steps)
            ready[k, rows, :] = (pre[k, rows, :] * scale).astype(ready.dtype)
            move = pltpu.make_async_copy(
                ready.at[k, rows], out_ref.at[c, rows], sems.at[steps * k + j]
            )
            move.start()
            moves.append(move)
    for move in moves:
        move.wait()


def apply_roots(rep, grad, left_root, right_root, right_oth):
    strips, block, strip = grad.shape
    steps = 4
    out = pltpu.HBM(grad.shape, jnp.bfloat16)
    return pl.pallas_call(
        functools.partial(root_kernel, steps),
        grid_spec=pltpu.PrefetchScalarGridSpec(
            num_scalar_prefetch=1,
            grid=(1,),
            in_specs=[
                pl.BlockSpec(memory_space=pltpu.VMEM),
                pl.BlockSpec(memory_space=pltpu.HBM),
                pl.BlockSpec(memory_space=pltpu.VMEM),
                pl.BlockSpec(memory_space=pltpu.HBM),
            ],
            out_specs=[pl.BlockSpec(memory_space=pltpu.HBM)] * 2,
            scratch_shapes=[
                pltpu.VMEM((block, strip), jnp.bfloat16),
                pltpu.VMEM((block, block), jnp.bfloat16),
                pltpu.VMEM(grad.shape, jnp.bfloat16),
                pltpu.VMEM(grad.shape, jnp.float32),
                pltpu.VMEM(grad.shape, jnp.bfloat16),
                pltpu.SemaphoreType.DMA((strips * steps,)),
                pltpu.SemaphoreType.DMA((2,)),
                pltpu.SemaphoreType.DMA,
            ],
        ),
        out_shape=[out, out],
        compiler_params=params(),
        cost_estimate=cost(4 * block**3, 8 * block * block),
        name="roots",
    )(rep, in_vmem(grad), in_hbm(right_root), in_vmem(right_oth), in_hbm(left_root))


def gram_kernel(steps, rep_ref, own_ref, oth_ref, left_out, right_out):
    i = pl.program_id(0)
    rep = rep_ref[0]

    def form(grad_ref):
        strips, _, strip = grad_ref.shape
        tile = strip // steps
        begin = pl.multiple_of((i % steps) * tile, tile)
        rows = pl.ds(pl.multiple_of(rep * strip + begin, tile), tile)
        left = lax.dot_general(
            grad_ref[0, rows, :], grad_ref[0], NT, preferred_element_type=jnp.float32
        )
        for k in range(1, strips):
            left += lax.dot_general(
                grad_ref[k, rows, :], grad_ref[k], NT, preferred_element_type=jnp.float32
            )
        left_out[0] = left
        columns = grad_ref[rep, :, pl.ds(begin, tile)]
        for k in range(strips):
            right_out[0, :, k * strip : (k + 1) * strip] = lax.dot_general(
                columns, grad_ref[k], TN, preferred_element_type=jnp.float32
            )

    pl.when(i < steps)(lambda: form(own_ref))
    pl.when(i >= steps)(lambda: form(oth_ref))


def grams(rep, own, oth):
    slots, block, strip = own.shape
    steps = 2
    tile = strip // steps
    out = jax.ShapeDtypeStruct((slots, strip, block), jnp.float32)

    def where(i, rep):
        return (jnp.where(i < steps, rep[0], 1 - rep[0]), i % steps, 0)

    return pl.pallas_call(
        functools.partial(gram_kernel, steps),
        grid_spec=pltpu.PrefetchScalarGridSpec(
            num_scalar_prefetch=1,
            grid=(2 * steps,),
            in_specs=[pl.BlockSpec(own.shape, lambda i, rep: (0, 0, 0))] * 2,
            out_specs=[pl.BlockSpec((1, tile, block), where)] * 2,
        ),
        out_shape=[out, out],
        compiler_params=params(),
        cost_estimate=cost(8 * block * block * strip, 24 * block * strip),
        name="grams",
    )(rep, own, oth)


def place_kernel(source_ref, row_ref, pieces_ref, out_ref, sem):
    piece = pieces_ref.shape[1]

    def start(b, carry):
        row = pl.multiple_of(row_ref[b], piece)
        pltpu.make_async_copy(
            pieces_ref.at[source_ref[b]], out_ref.at[pl.ds(row, piece), :], sem
        ).start()
        return carry

    lax.fori_loop(0, row_ref.shape[0], start, 0, unroll=4)
    pltpu.make_async_copy(out_ref, out_ref, sem).wait()


def place_rows(rows, source, row, pieces):
    _, piece, strip = pieces.shape
    return pl.pallas_call(
        place_kernel,
        grid_spec=pltpu.PrefetchScalarGridSpec(
            num_scalar_prefetch=2,
            grid=(1,),
            in_specs=[pl.BlockSpec(memory_space=pl.ANY)],
            out_specs=pl.BlockSpec(memory_space=pl.ANY),
            scratch_shapes=[pltpu.SemaphoreType.DMA],
        ),
        out_shape=jax.ShapeDtypeStruct((rows, strip), pieces.dtype),
        compiler_params=params(),
        cost_estimate=cost(0, 4 * rows * strip),
        name="place",
    )(source, row, pieces)


def local(gradients, owner_table, offsets, left_root, right_root):
    shard_count = lax.axis_size("shard")
    slots, block = left_root.shape[:2]
    strip = right_root.shape[2]
    piece = block // shard_count
    rows = gradients.shape[1]
    block_ids = jnp.arange(offsets.shape[0], dtype=jnp.int32)
    me = lax.axis_index("rep").astype(jnp.int32)
    rep = me.reshape(1)

    send = take_strip(strip, 1 - rep, gradients[0])
    theirs = lax.ppermute(send, "rep", SWAP)
    send, whole = lax.optimization_barrier((send, gradients[0]))
    mine = take_strip(strip, rep, whole)
    same_owner = owner_table[:, None] == owner_table[None, :]
    before = block_ids[:, None] < block_ids[None, :]
    rank = jnp.sum(jnp.where(same_owner & before, 1, 0), axis=0).astype(jnp.int32)
    holder_id = rank * shard_count + owner_table
    holder_ids = jnp.arange(slots * shard_count, dtype=jnp.int32)
    held = holder_id[:, None] == holder_ids[None, :]
    place = jnp.sum(jnp.where(held, (offsets // piece)[:, None] + 1, 0), axis=0) - 1
    place = place.astype(jnp.int32)

    def exchange(x):
        return lax.all_to_all(x, BOTH, split_axis=0, concat_axis=0, tiled=True)

    packed = pack(slots * shard_count, piece, place, mine, theirs)
    packed, right_later = lax.optimization_barrier((packed, right_root))
    right_oth = lax.ppermute(
        lax.dynamic_slice_in_dim(right_later, 1 - me, 1, 0), "rep", SWAP
    )
    right_oth = fetch(right_oth)
    grad = exchange(packed).reshape(slots, block, strip)
    update, grad = apply_roots(rep, grad, left_root, right_root, right_oth)
    update, grad = lax.optimization_barrier((update, grad))
    back = exchange(update.reshape(packed.shape))
    grad_other = lax.ppermute(grad, "rep", SWAP)
    gram_left, gram_right = grams(rep, grad, grad_other)
    holder_id, gram_left = lax.optimization_barrier((holder_id, gram_left))
    return place_rows(rows, holder_id, offsets, back), gram_left, gram_right


def solution(mesh):
    in_specs = (P("rep", "shard", None), P(), P(), P("shard", None, None), P("shard", None, "rep"))
    out_specs = (P("shard", "rep"), P("shard", "rep", None), P("shard", "rep", None))
    return jax.shard_map(local, mesh=mesh, in_specs=in_specs, out_specs=out_specs, check_vma=False)
```

```python
import functools

import jax
import jax.numpy as jnp
from jax import lax
from jax.experimental import pallas as pl
from jax.experimental.pallas import tpu as pltpu
from jax.sharding import PartitionSpec as P

EPSILON = 1e-06
VMEM_BYTES = 24 * 1024 * 1024
NT = (((1,), (1,)), ((), ()))
TN = (((0,), (0,)), ((), ()))
SWAP = [(0, 1), (1, 0)]
BOTH = ("rep", "shard")


def cost(flops, nbytes):
    return pl.CostEstimate(flops=flops, bytes_accessed=nbytes, transcendentals=0)


def params():
    return pltpu.CompilerParams(vmem_limit_bytes=VMEM_BYTES)


def in_vmem(x):
    return pltpu.with_memory_space_constraint(x, pltpu.VMEM)


def in_hbm(x):
    return pltpu.with_memory_space_constraint(x, pltpu.HBM)


def strip_kernel(steps, which_ref, rows_ref, strip_ref, sems):
    rows, strip = strip_ref.shape
    columns = pl.ds(pl.multiple_of(which_ref[0] * strip, strip), strip)
    moves = []
    for k in range(steps):
        here = pl.ds(k * (rows // steps), rows // steps)
        move = pltpu.make_async_copy(rows_ref.at[here, columns], strip_ref.at[here], sems.at[k])
        move.start()
        moves.append(move)
    for move in moves:
        move.wait()


def take_strip(strip, which, gradients):
    rows = gradients.shape[0]
    steps = 4
    return pl.pallas_call(
        functools.partial(strip_kernel, steps),
        grid_spec=pltpu.PrefetchScalarGridSpec(
            num_scalar_prefetch=1,
            grid=(1,),
            in_specs=[pl.BlockSpec(memory_space=pltpu.HBM)],
            out_specs=pl.BlockSpec(memory_space=pltpu.VMEM),
            scratch_shapes=[pltpu.SemaphoreType.DMA((steps,))],
        ),
        out_shape=pltpu.VMEM((rows, strip), gradients.dtype),
        compiler_params=params(),
        cost_estimate=cost(0, 4 * rows * strip),
        name="strip",
    )(which, in_hbm(gradients))


def fetch_kernel(right_ref, right_out, sems):
    moves = []
    for k in range(sems.shape[0]):
        count = right_out.shape[0] // sems.shape[0]
        rows = pl.ds(k * count, count)
        move = pltpu.make_async_copy(right_ref.at[0, rows], right_out.at[rows], sems.at[k])
        move.start()
        moves.append(move)
    for move in moves:
        move.wait()


def fetch(right):
    return pl.pallas_call(
        fetch_kernel,
        in_specs=[pl.BlockSpec(memory_space=pltpu.HBM)],
        out_specs=pl.BlockSpec(memory_space=pltpu.VMEM),
        scratch_shapes=[pltpu.SemaphoreType.DMA((2,))],
        out_shape=pltpu.VMEM(right.shape[1:], right.dtype),
        compiler_params=params(),
        cost_estimate=cost(0, 4 * right.size),
        name="fetch",
    )(in_hbm(right))


def pack_kernel(slot_ref, mine_ref, theirs_ref, out_ref, total, sem):
    piece = out_ref.shape[1]

    def step(i, carry):
        rows = pl.ds(pl.multiple_of(i * piece, piece), piece)
        total[rows, :] = mine_ref[rows, :] + theirs_ref[rows, :]
        pltpu.make_async_copy(total.at[rows], out_ref.at[slot_ref[i]], sem).start()
        return carry

    lax.fori_loop(0, total.shape[0] // piece, step, 0, unroll=16)
    pltpu.make_async_copy(total, total, sem).wait()


def pack(pieces, piece, slot_of_row, mine, theirs):
    rows, strip = theirs.shape
    return pl.pallas_call(
        pack_kernel,
        grid_spec=pltpu.PrefetchScalarGridSpec(
            num_scalar_prefetch=1,
            grid=(1,),
            in_specs=[pl.BlockSpec(memory_space=pltpu.VMEM)] * 2,
            out_specs=pl.BlockSpec(memory_space=pltpu.HBM),
            scratch_shapes=[
                pltpu.VMEM((rows, strip), theirs.dtype),
                pltpu.SemaphoreType.DMA,
            ],
        ),
        out_shape=pltpu.HBM((pieces, piece, strip), theirs.dtype),
        compiler_params=params(),
        cost_estimate=cost(rows * strip, 2 * rows * strip),
        name="pack",
    )(slot_of_row, in_vmem(mine), in_vmem(theirs))


def root_kernel(
    steps,
    rep_ref,
    grad_ref,
    right_ref,
    right_oth,
    left_ref,
    out_ref,
    kept_ref,
    right_own,
    left,
    half,
    pre,
    ready,
    sems,
    in_sems,
    kept_sem,
):
    rep = rep_ref[0]
    strips, block, strip = half.shape
    fetch_right = pltpu.make_async_copy(right_ref.at[rep], right_own, in_sems.at[0])
    fetch_left = pltpu.make_async_copy(left_ref.at[rep], left, in_sems.at[1])
    keep = pltpu.make_async_copy(grad_ref, kept_ref, kept_sem)
    fetch_right.start()
    fetch_left.start()
    for k, right in ((1, right_oth), (0, right_own)):
        if k == 0:
            fetch_right.wait()
        wide = jnp.concatenate([grad_ref[j] for j in range(strips)], axis=1)
        acc = jnp.dot(wide, right[...], preferred_element_type=jnp.float32)
        half[k] = acc.astype(half.dtype)
    grad_sq = jnp.zeros((1, strip), jnp.float32)
    for k in range(strips):
        value = grad_ref[k].astype(jnp.float32)
        grad_sq += jnp.sum(value * value, axis=0, keepdims=True)
    fetch_left.wait()
    keep.start()
    pre_sq = jnp.zeros((1, strip), jnp.float32)
    for k in range(strips):
        value = jnp.dot(left[...], half[k], preferred_element_type=jnp.float32)
        pre[k] = value
        pre_sq += jnp.sum(value * value, axis=0, keepdims=True)
    entries = float(block * block)
    top = jnp.full((8, 128), jnp.sum(grad_sq), jnp.float32) / entries
    bottom = jnp.full((8, 128), jnp.sum(pre_sq), jnp.float32) / entries + EPSILON
    scale = jnp.sqrt(top / bottom)[0:1, 0:1]
    moves = [keep]
    for k, c in ((0, rep), (1, 1 - rep)):
        for j in range(steps):
            rows = pl.ds(j * (block // steps), block // steps)
            ready[k, rows, :] = (pre[k, rows, :] * scale).astype(ready.dtype)
            move = pltpu.make_async_copy(
                ready.at[k, rows], out_ref.at[c, rows], sems.at[steps * k + j]
            )
            move.start()
            moves.append(move)
    for move in moves:
        move.wait()


def apply_roots(rep, grad, left_root, right_root, right_oth):
    strips, block, strip = grad.shape
    steps = 4
    out = pltpu.HBM(grad.shape, jnp.bfloat16)
    return pl.pallas_call(
        functools.partial(root_kernel, steps),
        grid_spec=pltpu.PrefetchScalarGridSpec(
            num_scalar_prefetch=1,
            grid=(1,),
            in_specs=[
                pl.BlockSpec(memory_space=pltpu.VMEM),
                pl.BlockSpec(memory_space=pltpu.HBM),
                pl.BlockSpec(memory_space=pltpu.VMEM),
                pl.BlockSpec(memory_space=pltpu.HBM),
            ],
            out_specs=[pl.BlockSpec(memory_space=pltpu.HBM)] * 2,
            scratch_shapes=[
                pltpu.VMEM((block, strip), jnp.bfloat16),
                pltpu.VMEM((block, block), jnp.bfloat16),
                pltpu.VMEM(grad.shape, jnp.bfloat16),
                pltpu.VMEM(grad.shape, jnp.float32),
                pltpu.VMEM(grad.shape, jnp.bfloat16),
                pltpu.SemaphoreType.DMA((strips * steps,)),
                pltpu.SemaphoreType.DMA((2,)),
                pltpu.SemaphoreType.DMA,
            ],
        ),
        out_shape=[out, out],
        compiler_params=params(),
        cost_estimate=cost(4 * block**3, 8 * block * block),
        name="roots",
    )(rep, in_vmem(grad), in_hbm(right_root), in_vmem(right_oth), in_hbm(left_root))


def gram_kernel(steps, rep_ref, held_ref, own_ref, oth_ref, left_out, right_out):
    i = pl.program_id(0)
    rep = rep_ref[0]

    def form(grad_ref, slot):
        held = held_ref[slot] != 0
        strips, _, strip = grad_ref.shape
        tile = strip // steps
        begin = pl.multiple_of((i % steps) * tile, tile)
        rows = pl.ds(pl.multiple_of(rep * strip + begin, tile), tile)
        left = lax.dot_general(
            grad_ref[0, rows, :], grad_ref[0], NT, preferred_element_type=jnp.float32
        )
        for k in range(1, strips):
            left += lax.dot_general(
                grad_ref[k, rows, :], grad_ref[k], NT, preferred_element_type=jnp.float32
            )
        left_out[0] = jnp.where(held, left, 0.0)
        columns = grad_ref[rep, :, pl.ds(begin, tile)]
        for k in range(strips):
            right = lax.dot_general(
                columns, grad_ref[k], TN, preferred_element_type=jnp.float32
            )
            right_out[0, :, k * strip : (k + 1) * strip] = jnp.where(held, right, 0.0)

    pl.when(i < steps)(lambda: form(own_ref, rep))
    pl.when(i >= steps)(lambda: form(oth_ref, 1 - rep))


def grams(rep, held, own, oth):
    slots, block, strip = own.shape
    steps = 2
    tile = strip // steps
    out = jax.ShapeDtypeStruct((slots, strip, block), jnp.float32)

    def where(i, rep, held):
        return (jnp.where(i < steps, rep[0], 1 - rep[0]), i % steps, 0)

    return pl.pallas_call(
        functools.partial(gram_kernel, steps),
        grid_spec=pltpu.PrefetchScalarGridSpec(
            num_scalar_prefetch=2,
            grid=(2 * steps,),
            in_specs=[pl.BlockSpec(own.shape, lambda i, rep, held: (0, 0, 0))] * 2,
            out_specs=[pl.BlockSpec((1, tile, block), where)] * 2,
        ),
        out_shape=[out, out],
        compiler_params=params(),
        cost_estimate=cost(8 * block * block * strip, 24 * block * strip),
        name="grams",
    )(rep, held, own, oth)


def place_kernel(source_ref, row_ref, pieces_ref, out_ref, sem):
    piece = pieces_ref.shape[1]

    def start(b, carry):
        row = pl.multiple_of(row_ref[b], piece)
        pltpu.make_async_copy(
            pieces_ref.at[source_ref[b]], out_ref.at[pl.ds(row, piece), :], sem
        ).start()
        return carry

    lax.fori_loop(0, row_ref.shape[0], start, 0, unroll=4)
    pltpu.make_async_copy(out_ref, out_ref, sem).wait()


def place_rows(rows, source, row, pieces):
    _, piece, strip = pieces.shape
    return pl.pallas_call(
        place_kernel,
        grid_spec=pltpu.PrefetchScalarGridSpec(
            num_scalar_prefetch=2,
            grid=(1,),
            in_specs=[pl.BlockSpec(memory_space=pl.ANY)],
            out_specs=pl.BlockSpec(memory_space=pl.ANY),
            scratch_shapes=[pltpu.SemaphoreType.DMA],
        ),
        out_shape=jax.ShapeDtypeStruct((rows, strip), pieces.dtype),
        compiler_params=params(),
        cost_estimate=cost(0, 4 * rows * strip),
        name="place",
    )(source, row, pieces)


def local(gradients, owner_table, offsets, left_root, right_root):
    shard_count = lax.axis_size("shard")
    slots, block = left_root.shape[:2]
    strip = right_root.shape[2]
    piece = block // shard_count
    rows = gradients.shape[1]
    block_ids = jnp.arange(offsets.shape[0], dtype=jnp.int32)
    me = lax.axis_index("rep").astype(jnp.int32)
    rep = me.reshape(1)

    send = take_strip(strip, 1 - rep, gradients[0])
    theirs = lax.ppermute(send, "rep", SWAP)
    send, whole = lax.optimization_barrier((send, gradients[0]))
    mine = take_strip(strip, rep, whole)
    same_owner = owner_table[:, None] == owner_table[None, :]
    before = block_ids[:, None] < block_ids[None, :]
    rank = jnp.sum(jnp.where(same_owner & before, 1, 0), axis=0).astype(jnp.int32)
    holder_id = rank * shard_count + owner_table
    at_row = (offsets // piece)[:, None] == block_ids[None, :]
    slot_of_row = jnp.sum(jnp.where(at_row, holder_id[:, None], 0), axis=0).astype(jnp.int32)
    my_slots = jnp.arange(slots, dtype=jnp.int32) * shard_count + lax.axis_index("shard")
    held = jnp.sum(jnp.where(holder_id[:, None] == my_slots[None, :], 1, 0), axis=0)
    held = held.astype(jnp.int32)

    def exchange(x):
        return lax.all_to_all(x, BOTH, split_axis=0, concat_axis=0, tiled=True)

    packed = pack(slots * shard_count, piece, slot_of_row, mine, theirs)
    packed, right_later = lax.optimization_barrier((packed, right_root))
    right_oth = lax.ppermute(
        lax.dynamic_slice_in_dim(right_later, 1 - me, 1, 0), "rep", SWAP
    )
    right_oth = fetch(right_oth)
    grad = exchange(packed).reshape(slots, block, strip)
    update, grad = apply_roots(rep, grad, left_root, right_root, right_oth)
    update, grad = lax.optimization_barrier((update, grad))
    back = exchange(update.reshape(packed.shape))
    grad_other = lax.ppermute(grad, "rep", SWAP)
    gram_left, gram_right = grams(rep, held, grad, grad_other)
    holder_id, gram_left = lax.optimization_barrier((holder_id, gram_left))
    return place_rows(rows, holder_id, offsets, back), gram_left, gram_right


def solution(mesh):
    in_specs = (P("rep", "shard", None), P(), P(), P("shard", None, None), P("shard", None, "rep"))
    out_specs = (P("shard", "rep"), P("shard", "rep", None), P("shard", "rep", None))
    return jax.shard_map(local, mesh=mesh, in_specs=in_specs, out_specs=out_specs, check_vma=False)
```

```python
import functools

import jax
import jax.numpy as jnp
from jax import lax
from jax.experimental import pallas as pl
from jax.experimental.pallas import tpu as pltpu
from jax.sharding import PartitionSpec as P

EPSILON = 1e-06
VMEM_BYTES = 24 * 1024 * 1024
NT = (((1,), (1,)), ((), ()))
TN = (((0,), (0,)), ((), ()))
SWAP = [(0, 1), (1, 0)]
BOTH = ("rep", "shard")


def cost(flops, nbytes):
    return pl.CostEstimate(flops=flops, bytes_accessed=nbytes, transcendentals=0)


def params():
    return pltpu.CompilerParams(vmem_limit_bytes=VMEM_BYTES)


def in_vmem(x):
    return pltpu.with_memory_space_constraint(x, pltpu.VMEM)


def in_hbm(x):
    return pltpu.with_memory_space_constraint(x, pltpu.HBM)


def strip_kernel(steps, which_ref, rows_ref, strip_ref, sems):
    rows, strip = strip_ref.shape
    columns = pl.ds(pl.multiple_of(which_ref[0] * strip, strip), strip)
    moves = []
    for k in range(steps):
        here = pl.ds(k * (rows // steps), rows // steps)
        move = pltpu.make_async_copy(rows_ref.at[here, columns], strip_ref.at[here], sems.at[k])
        move.start()
        moves.append(move)
    for move in moves:
        move.wait()


def take_strip(strip, which, gradients):
    rows = gradients.shape[0]
    steps = 4
    return pl.pallas_call(
        functools.partial(strip_kernel, steps),
        grid_spec=pltpu.PrefetchScalarGridSpec(
            num_scalar_prefetch=1,
            grid=(1,),
            in_specs=[pl.BlockSpec(memory_space=pltpu.HBM)],
            out_specs=pl.BlockSpec(memory_space=pltpu.VMEM),
            scratch_shapes=[pltpu.SemaphoreType.DMA((steps,))],
        ),
        out_shape=pltpu.VMEM((rows, strip), gradients.dtype),
        compiler_params=params(),
        cost_estimate=cost(0, 4 * rows * strip),
        name="strip",
    )(which, in_hbm(gradients))


def fetch_kernel(right_ref, right_out, sems):
    moves = []
    for k in range(sems.shape[0]):
        count = right_out.shape[0] // sems.shape[0]
        rows = pl.ds(k * count, count)
        move = pltpu.make_async_copy(right_ref.at[0, rows], right_out.at[rows], sems.at[k])
        move.start()
        moves.append(move)
    for move in moves:
        move.wait()


def fetch(right):
    return pl.pallas_call(
        fetch_kernel,
        in_specs=[pl.BlockSpec(memory_space=pltpu.HBM)],
        out_specs=pl.BlockSpec(memory_space=pltpu.VMEM),
        scratch_shapes=[pltpu.SemaphoreType.DMA((2,))],
        out_shape=pltpu.VMEM(right.shape[1:], right.dtype),
        compiler_params=params(),
        cost_estimate=cost(0, 4 * right.size),
        name="fetch",
    )(in_hbm(right))


def pack_kernel(slot_ref, mine_ref, theirs_ref, out_ref, total, sem):
    piece = out_ref.shape[1]

    def step(i, carry):
        rows = pl.ds(pl.multiple_of(i * piece, piece), piece)
        total[rows, :] = mine_ref[rows, :] + theirs_ref[rows, :]
        pltpu.make_async_copy(total.at[rows], out_ref.at[slot_ref[i]], sem).start()
        return carry

    lax.fori_loop(0, total.shape[0] // piece, step, 0, unroll=16)
    pltpu.make_async_copy(total, total, sem).wait()


def pack(pieces, piece, slot_of_row, mine, theirs):
    rows, strip = theirs.shape
    return pl.pallas_call(
        pack_kernel,
        grid_spec=pltpu.PrefetchScalarGridSpec(
            num_scalar_prefetch=1,
            grid=(1,),
            in_specs=[pl.BlockSpec(memory_space=pltpu.VMEM)] * 2,
            out_specs=pl.BlockSpec(memory_space=pltpu.HBM),
            scratch_shapes=[
                pltpu.VMEM((rows, strip), theirs.dtype),
                pltpu.SemaphoreType.DMA,
            ],
        ),
        out_shape=pltpu.HBM((pieces, piece, strip), theirs.dtype),
        compiler_params=params(),
        cost_estimate=cost(rows * strip, 2 * rows * strip),
        name="pack",
    )(slot_of_row, in_vmem(mine), in_vmem(theirs))


def root_kernel(
    steps,
    rep_ref,
    grad_ref,
    right_ref,
    right_oth,
    left_ref,
    out_ref,
    kept_ref,
    right_own,
    left,
    half,
    pre,
    ready,
    sems,
    in_sems,
    kept_sem,
):
    rep = rep_ref[0]
    strips, block, strip = half.shape
    fetch_right = pltpu.make_async_copy(right_ref.at[rep], right_own, in_sems.at[0])
    fetch_left = pltpu.make_async_copy(left_ref.at[rep], left, in_sems.at[1])
    keep = pltpu.make_async_copy(grad_ref, kept_ref, kept_sem)
    fetch_right.start()
    fetch_left.start()
    for k, right in ((1, right_oth), (0, right_own)):
        if k == 0:
            fetch_right.wait()
        wide = jnp.concatenate([grad_ref[j] for j in range(strips)], axis=1)
        acc = jnp.dot(wide, right[...], preferred_element_type=jnp.float32)
        half[k] = acc.astype(half.dtype)
    grad_sq = jnp.zeros((1, strip), jnp.float32)
    for k in range(strips):
        value = grad_ref[k].astype(jnp.float32)
        grad_sq += jnp.sum(value * value, axis=0, keepdims=True)
    fetch_left.wait()
    keep.start()
    pre_sq = jnp.zeros((1, strip), jnp.float32)
    for k in range(strips):
        value = jnp.dot(left[...], half[k], preferred_element_type=jnp.float32)
        pre[k] = value
        pre_sq += jnp.sum(value * value, axis=0, keepdims=True)
    entries = float(block * block)
    top = jnp.full((8, 128), jnp.sum(grad_sq), jnp.float32) / entries
    bottom = jnp.full((8, 128), jnp.sum(pre_sq), jnp.float32) / entries + EPSILON
    scale = jnp.sqrt(top / bottom)[0:1, 0:1]
    moves = [keep]
    for k, c in ((0, rep), (1, 1 - rep)):
        for j in range(steps):
            rows = pl.ds(j * (block // steps), block // steps)
            ready[k, rows, :] = (pre[k, rows, :] * scale).astype(ready.dtype)
            move = pltpu.make_async_copy(
                ready.at[k, rows], out_ref.at[c, rows], sems.at[steps * k + j]
            )
            move.start()
            moves.append(move)
    for move in moves:
        move.wait()


def apply_roots(rep, grad, left_root, right_root, right_oth):
    strips, block, strip = grad.shape
    steps = 4
    out = pltpu.HBM(grad.shape, jnp.bfloat16)
    return pl.pallas_call(
        functools.partial(root_kernel, steps),
        grid_spec=pltpu.PrefetchScalarGridSpec(
            num_scalar_prefetch=1,
            grid=(1,),
            in_specs=[
                pl.BlockSpec(memory_space=pltpu.VMEM),
                pl.BlockSpec(memory_space=pltpu.HBM),
                pl.BlockSpec(memory_space=pltpu.VMEM),
                pl.BlockSpec(memory_space=pltpu.HBM),
            ],
            out_specs=[pl.BlockSpec(memory_space=pltpu.HBM)] * 2,
            scratch_shapes=[
                pltpu.VMEM((block, strip), jnp.bfloat16),
                pltpu.VMEM((block, block), jnp.bfloat16),
                pltpu.VMEM(grad.shape, jnp.bfloat16),
                pltpu.VMEM(grad.shape, jnp.float32),
                pltpu.VMEM(grad.shape, jnp.bfloat16),
                pltpu.SemaphoreType.DMA((strips * steps,)),
                pltpu.SemaphoreType.DMA((2,)),
                pltpu.SemaphoreType.DMA,
            ],
        ),
        out_shape=[out, out],
        compiler_params=params(),
        cost_estimate=cost(4 * block**3, 8 * block * block),
        name="roots",
    )(rep, in_vmem(grad), in_hbm(right_root), in_vmem(right_oth), in_hbm(left_root))


def gram_kernel(steps, rep_ref, slot_ref, held_ref, grad_ref, *rest):
    left_out, right_out = rest[-2:]
    strips, _, strip = grad_ref.shape
    tile = strip // steps
    rep = rep_ref[0]
    held = held_ref[slot_ref[0]] != 0
    begin = pl.multiple_of(pl.program_id(0) * tile, tile)
    rows = pl.ds(pl.multiple_of(rep * strip + begin, tile), tile)
    left = lax.dot_general(
        grad_ref[0, rows, :], grad_ref[0], NT, preferred_element_type=jnp.float32
    )
    for k in range(1, strips):
        left += lax.dot_general(
            grad_ref[k, rows, :], grad_ref[k], NT, preferred_element_type=jnp.float32
        )
    left_out[0] = jnp.where(held, left, 0.0)
    columns = grad_ref[rep, :, pl.ds(begin, tile)]
    for k in range(strips):
        right = lax.dot_general(columns, grad_ref[k], TN, preferred_element_type=jnp.float32)
        right_out[0, :, k * strip : (k + 1) * strip] = jnp.where(held, right, 0.0)


def grams(slots, rep, slot, held, grad, previous):
    strips, block, strip = grad.shape
    steps = 2
    tile = strip // steps
    out = jax.ShapeDtypeStruct((slots, strip, block), jnp.float32)

    def whole(i, rep, slot, held):
        return (0, 0, 0)

    def where(i, rep, slot, held):
        return (slot[0], i, 0)

    return pl.pallas_call(
        functools.partial(gram_kernel, steps),
        grid_spec=pltpu.PrefetchScalarGridSpec(
            num_scalar_prefetch=3,
            grid=(steps,),
            in_specs=[pl.BlockSpec(grad.shape, whole)]
            + [pl.BlockSpec(memory_space=pl.ANY)] * len(previous),
            out_specs=[pl.BlockSpec((1, tile, block), where)] * 2,
        ),
        out_shape=[out, out],
        input_output_aliases={4 + k: k for k in range(len(previous))},
        compiler_params=params(),
        cost_estimate=cost(4 * block * block * strip, 12 * block * strip),
        name="grams",
    )(rep, slot, held, grad, *previous)


def place_kernel(source_ref, row_ref, pieces_ref, out_ref, sem):
    piece = pieces_ref.shape[1]

    def start(b, carry):
        row = pl.multiple_of(row_ref[b], piece)
        pltpu.make_async_copy(
            pieces_ref.at[source_ref[b]], out_ref.at[pl.ds(row, piece), :], sem
        ).start()
        return carry

    lax.fori_loop(0, row_ref.shape[0], start, 0, unroll=4)
    pltpu.make_async_copy(out_ref, out_ref, sem).wait()


def place_rows(rows, source, row, pieces):
    _, piece, strip = pieces.shape
    return pl.pallas_call(
        place_kernel,
        grid_spec=pltpu.PrefetchScalarGridSpec(
            num_scalar_prefetch=2,
            grid=(1,),
            in_specs=[pl.BlockSpec(memory_space=pl.ANY)],
            out_specs=pl.BlockSpec(memory_space=pl.ANY),
            scratch_shapes=[pltpu.SemaphoreType.DMA],
        ),
        out_shape=jax.ShapeDtypeStruct((rows, strip), pieces.dtype),
        compiler_params=params(),
        cost_estimate=cost(0, 4 * rows * strip),
        name="place",
    )(source, row, pieces)


def local(gradients, owner_table, offsets, left_root, right_root):
    shard_count = lax.axis_size("shard")
    slots, block = left_root.shape[:2]
    strip = right_root.shape[2]
    piece = block // shard_count
    rows = gradients.shape[1]
    block_ids = jnp.arange(offsets.shape[0], dtype=jnp.int32)
    me = lax.axis_index("rep").astype(jnp.int32)
    rep = me.reshape(1)

    send = take_strip(strip, 1 - rep, gradients[0])
    theirs = lax.ppermute(send, "rep", SWAP)
    send, whole = lax.optimization_barrier((send, gradients[0]))
    mine = take_strip(strip, rep, whole)
    same_owner = owner_table[:, None] == owner_table[None, :]
    before = block_ids[:, None] < block_ids[None, :]
    rank = jnp.sum(jnp.where(same_owner & before, 1, 0), axis=0).astype(jnp.int32)
    holder_id = rank * shard_count + owner_table
    at_row = (offsets // piece)[:, None] == block_ids[None, :]
    slot_of_row = jnp.sum(jnp.where(at_row, holder_id[:, None], 0), axis=0).astype(jnp.int32)
    my_slots = jnp.arange(slots, dtype=jnp.int32) * shard_count + lax.axis_index("shard")
    held = jnp.sum(jnp.where(holder_id[:, None] == my_slots[None, :], 1, 0), axis=0)
    held = held.astype(jnp.int32)

    def exchange(x):
        return lax.all_to_all(x, BOTH, split_axis=0, concat_axis=0, tiled=True)

    packed = pack(slots * shard_count, piece, slot_of_row, mine, theirs)
    packed, right_later = lax.optimization_barrier((packed, right_root))
    right_oth = lax.ppermute(
        lax.dynamic_slice_in_dim(right_later, 1 - me, 1, 0), "rep", SWAP
    )
    right_oth = fetch(right_oth)
    grad = exchange(packed).reshape(slots, block, strip)
    update, grad = apply_roots(rep, grad, left_root, right_root, right_oth)
    update, grad = lax.optimization_barrier((update, grad))
    back = exchange(update.reshape(packed.shape))
    grad_other = lax.ppermute(grad, "rep", SWAP)
    gram = grams(slots, rep, rep, held, grad, ())
    gram_left, gram_right = grams(slots, rep, 1 - rep, held, grad_other, tuple(gram))
    holder_id, gram_left = lax.optimization_barrier((holder_id, gram_left))
    return place_rows(rows, holder_id, offsets, back), gram_left, gram_right


def solution(mesh):
    in_specs = (P("rep", "shard", None), P(), P(), P("shard", None, None), P("shard", None, "rep"))
    out_specs = (P("shard", "rep"), P("shard", "rep", None), P("shard", "rep", None))
    return jax.shard_map(local, mesh=mesh, in_specs=in_specs, out_specs=out_specs, check_vma=False)
```

```python
import functools

import jax
import jax.numpy as jnp
from jax import lax
from jax.experimental import pallas as pl
from jax.experimental.pallas import tpu as pltpu
from jax.sharding import PartitionSpec as P

EPSILON = 1e-06
VMEM_BYTES = 24 * 1024 * 1024
NT = (((1,), (1,)), ((), ()))
TN = (((0,), (0,)), ((), ()))
SWAP = [(0, 1), (1, 0)]
BOTH = ("rep", "shard")


def cost(flops, nbytes):
    return pl.CostEstimate(flops=flops, bytes_accessed=nbytes, transcendentals=0)


def params():
    return pltpu.CompilerParams(vmem_limit_bytes=VMEM_BYTES)


def in_vmem(x):
    return pltpu.with_memory_space_constraint(x, pltpu.VMEM)


def in_hbm(x):
    return pltpu.with_memory_space_constraint(x, pltpu.HBM)


def strip_kernel(steps, which_ref, rows_ref, strip_ref, sems):
    rows, strip = strip_ref.shape
    columns = pl.ds(pl.multiple_of(which_ref[0] * strip, strip), strip)
    moves = []
    for k in range(steps):
        here = pl.ds(k * (rows // steps), rows // steps)
        move = pltpu.make_async_copy(rows_ref.at[here, columns], strip_ref.at[here], sems.at[k])
        move.start()
        moves.append(move)
    for move in moves:
        move.wait()


def take_strip(strip, which, gradients):
    rows = gradients.shape[0]
    steps = 4
    return pl.pallas_call(
        functools.partial(strip_kernel, steps),
        grid_spec=pltpu.PrefetchScalarGridSpec(
            num_scalar_prefetch=1,
            grid=(1,),
            in_specs=[pl.BlockSpec(memory_space=pltpu.HBM)],
            out_specs=pl.BlockSpec(memory_space=pltpu.VMEM),
            scratch_shapes=[pltpu.SemaphoreType.DMA((steps,))],
        ),
        out_shape=pltpu.VMEM((rows, strip), gradients.dtype),
        compiler_params=params(),
        cost_estimate=cost(0, 4 * rows * strip),
        name="strip",
    )(which, in_hbm(gradients))


def fetch_kernel(right_ref, right_out, sems):
    moves = []
    for k in range(sems.shape[0]):
        count = right_out.shape[0] // sems.shape[0]
        rows = pl.ds(k * count, count)
        move = pltpu.make_async_copy(right_ref.at[0, rows], right_out.at[rows], sems.at[k])
        move.start()
        moves.append(move)
    for move in moves:
        move.wait()


def fetch(right):
    return pl.pallas_call(
        fetch_kernel,
        in_specs=[pl.BlockSpec(memory_space=pltpu.HBM)],
        out_specs=pl.BlockSpec(memory_space=pltpu.VMEM),
        scratch_shapes=[pltpu.SemaphoreType.DMA((2,))],
        out_shape=pltpu.VMEM(right.shape[1:], right.dtype),
        compiler_params=params(),
        cost_estimate=cost(0, 4 * right.size),
        name="fetch",
    )(in_hbm(right))


def pack_kernel(slot_ref, mine_ref, theirs_ref, out_ref, total, sem):
    piece = out_ref.shape[1]

    def step(i, carry):
        rows = pl.ds(pl.multiple_of(i * piece, piece), piece)
        total[rows, :] = mine_ref[rows, :] + theirs_ref[rows, :]
        pltpu.make_async_copy(total.at[rows], out_ref.at[slot_ref[i]], sem).start()
        return carry

    lax.fori_loop(0, total.shape[0] // piece, step, 0, unroll=16)
    pltpu.make_async_copy(total, total, sem).wait()


def pack(pieces, piece, slot_of_row, mine, theirs):
    rows, strip = theirs.shape
    return pl.pallas_call(
        pack_kernel,
        grid_spec=pltpu.PrefetchScalarGridSpec(
            num_scalar_prefetch=1,
            grid=(1,),
            in_specs=[pl.BlockSpec(memory_space=pltpu.VMEM)] * 2,
            out_specs=pl.BlockSpec(memory_space=pltpu.HBM),
            scratch_shapes=[
                pltpu.VMEM((rows, strip), theirs.dtype),
                pltpu.SemaphoreType.DMA,
            ],
        ),
        out_shape=pltpu.HBM((pieces, piece, strip), theirs.dtype),
        compiler_params=params(),
        cost_estimate=cost(rows * strip, 2 * rows * strip),
        name="pack",
    )(slot_of_row, in_vmem(mine), in_vmem(theirs))


def root_kernel(
    steps,
    rep_ref,
    grad_ref,
    right_ref,
    right_oth,
    left_ref,
    out_ref,
    kept_ref,
    right_own,
    left,
    half,
    pre,
    ready,
    sems,
    in_sems,
    kept_sem,
):
    rep = rep_ref[0]
    strips, block, strip = half.shape
    fetch_right = pltpu.make_async_copy(right_ref.at[rep], right_own, in_sems.at[0])
    fetch_left = pltpu.make_async_copy(left_ref.at[rep], left, in_sems.at[1])
    keep = pltpu.make_async_copy(grad_ref, kept_ref, kept_sem)
    fetch_right.start()
    fetch_left.start()
    for k, right in ((1, right_oth), (0, right_own)):
        if k == 0:
            grad_sq = jnp.zeros((1, strip), jnp.float32)
            for j in range(strips):
                value = grad_ref[j].astype(jnp.float32)
                grad_sq += jnp.sum(value * value, axis=0, keepdims=True)
            fetch_right.wait()
        wide = jnp.concatenate([grad_ref[j] for j in range(strips)], axis=1)
        acc = jnp.dot(wide, right[...], preferred_element_type=jnp.float32)
        half[k] = acc.astype(half.dtype)
    fetch_left.wait()
    keep.start()
    pre_sq = jnp.zeros((1, strip), jnp.float32)
    for k in range(strips):
        value = jnp.dot(left[...], half[k], preferred_element_type=jnp.float32)
        pre[k] = value
        pre_sq += jnp.sum(value * value, axis=0, keepdims=True)
    entries = float(block * block)
    top = jnp.full((8, 128), jnp.sum(grad_sq), jnp.float32) / entries
    bottom = jnp.full((8, 128), jnp.sum(pre_sq), jnp.float32) / entries + EPSILON
    scale = jnp.sqrt(top / bottom)[0:1, 0:1]
    moves = [keep]
    for k, c in ((0, rep), (1, 1 - rep)):
        for j in range(steps):
            rows = pl.ds(j * (block // steps), block // steps)
            ready[k, rows, :] = (pre[k, rows, :] * scale).astype(ready.dtype)
            move = pltpu.make_async_copy(
                ready.at[k, rows], out_ref.at[c, rows], sems.at[steps * k + j]
            )
            move.start()
            moves.append(move)
    for move in moves:
        move.wait()


def apply_roots(rep, grad, left_root, right_root, right_oth):
    strips, block, strip = grad.shape
    steps = 4
    out = pltpu.HBM(grad.shape, jnp.bfloat16)
    return pl.pallas_call(
        functools.partial(root_kernel, steps),
        grid_spec=pltpu.PrefetchScalarGridSpec(
            num_scalar_prefetch=1,
            grid=(1,),
            in_specs=[
                pl.BlockSpec(memory_space=pltpu.VMEM),
                pl.BlockSpec(memory_space=pltpu.HBM),
                pl.BlockSpec(memory_space=pltpu.VMEM),
                pl.BlockSpec(memory_space=pltpu.HBM),
            ],
            out_specs=[pl.BlockSpec(memory_space=pltpu.HBM)] * 2,
            scratch_shapes=[
                pltpu.VMEM((block, strip), jnp.bfloat16),
                pltpu.VMEM((block, block), jnp.bfloat16),
                pltpu.VMEM(grad.shape, jnp.bfloat16),
                pltpu.VMEM(grad.shape, jnp.float32),
                pltpu.VMEM(grad.shape, jnp.bfloat16),
                pltpu.SemaphoreType.DMA((strips * steps,)),
                pltpu.SemaphoreType.DMA((2,)),
                pltpu.SemaphoreType.DMA,
            ],
        ),
        out_shape=[out, out],
        compiler_params=params(),
        cost_estimate=cost(4 * block**3, 8 * block * block),
        name="roots",
    )(rep, in_vmem(grad), in_hbm(right_root), in_vmem(right_oth), in_hbm(left_root))


def gram_kernel(steps, rep_ref, held_ref, own_ref, oth_ref, left_out, right_out):
    i = pl.program_id(0)
    rep = rep_ref[0]

    def form(grad_ref, slot):
        held = held_ref[slot] != 0
        strips, _, strip = grad_ref.shape
        tile = strip // steps
        begin = pl.multiple_of((i % steps) * tile, tile)
        rows = pl.ds(pl.multiple_of(rep * strip + begin, tile), tile)
        left = lax.dot_general(
            grad_ref[0, rows, :], grad_ref[0], NT, preferred_element_type=jnp.float32
        )
        for k in range(1, strips):
            left += lax.dot_general(
                grad_ref[k, rows, :], grad_ref[k], NT, preferred_element_type=jnp.float32
            )
        left_out[0] = jnp.where(held, left, 0.0)
        columns = grad_ref[rep, :, pl.ds(begin, tile)]
        for k in range(strips):
            right = lax.dot_general(
                columns, grad_ref[k], TN, preferred_element_type=jnp.float32
            )
            right_out[0, :, k * strip : (k + 1) * strip] = jnp.where(held, right, 0.0)

    pl.when(i < steps)(lambda: form(own_ref, rep))
    pl.when(i >= steps)(lambda: form(oth_ref, 1 - rep))


def grams(rep, held, own, oth):
    slots, block, strip = own.shape
    steps = 2
    tile = strip // steps
    out = jax.ShapeDtypeStruct((slots, strip, block), jnp.float32)

    def where(i, rep, held):
        return (jnp.where(i < steps, rep[0], 1 - rep[0]), i % steps, 0)

    return pl.pallas_call(
        functools.partial(gram_kernel, steps),
        grid_spec=pltpu.PrefetchScalarGridSpec(
            num_scalar_prefetch=2,
            grid=(2 * steps,),
            in_specs=[pl.BlockSpec(own.shape, lambda i, rep, held: (0, 0, 0))] * 2,
            out_specs=[pl.BlockSpec((1, tile, block), where)] * 2,
        ),
        out_shape=[out, out],
        compiler_params=params(),
        cost_estimate=cost(8 * block * block * strip, 24 * block * strip),
        name="grams",
    )(rep, held, own, oth)


def place_kernel(source_ref, row_ref, pieces_ref, out_ref, sem):
    piece = pieces_ref.shape[1]

    def start(b, carry):
        row = pl.multiple_of(row_ref[b], piece)
        pltpu.make_async_copy(
            pieces_ref.at[source_ref[b]], out_ref.at[pl.ds(row, piece), :], sem
        ).start()
        return carry

    lax.fori_loop(0, row_ref.shape[0], start, 0, unroll=4)
    pltpu.make_async_copy(out_ref, out_ref, sem).wait()


def place_rows(rows, source, row, pieces):
    _, piece, strip = pieces.shape
    return pl.pallas_call(
        place_kernel,
        grid_spec=pltpu.PrefetchScalarGridSpec(
            num_scalar_prefetch=2,
            grid=(1,),
            in_specs=[pl.BlockSpec(memory_space=pl.ANY)],
            out_specs=pl.BlockSpec(memory_space=pl.ANY),
            scratch_shapes=[pltpu.SemaphoreType.DMA],
        ),
        out_shape=jax.ShapeDtypeStruct((rows, strip), pieces.dtype),
        compiler_params=params(),
        cost_estimate=cost(0, 4 * rows * strip),
        name="place",
    )(source, row, pieces)


def local(gradients, owner_table, offsets, left_root, right_root):
    shard_count = lax.axis_size("shard")
    slots, block = left_root.shape[:2]
    strip = right_root.shape[2]
    piece = block // shard_count
    rows = gradients.shape[1]
    block_ids = jnp.arange(offsets.shape[0], dtype=jnp.int32)
    me = lax.axis_index("rep").astype(jnp.int32)
    rep = me.reshape(1)

    send = take_strip(strip, 1 - rep, gradients[0])
    theirs = lax.ppermute(send, "rep", SWAP)
    send, whole = lax.optimization_barrier((send, gradients[0]))
    mine = take_strip(strip, rep, whole)
    same_owner = owner_table[:, None] == owner_table[None, :]
    before = block_ids[:, None] < block_ids[None, :]
    rank = jnp.sum(jnp.where(same_owner & before, 1, 0), axis=0).astype(jnp.int32)
    holder_id = rank * shard_count + owner_table
    at_row = (offsets // piece)[:, None] == block_ids[None, :]
    slot_of_row = jnp.sum(jnp.where(at_row, holder_id[:, None], 0), axis=0).astype(jnp.int32)
    my_slots = jnp.arange(slots, dtype=jnp.int32) * shard_count + lax.axis_index("shard")
    held = jnp.sum(jnp.where(holder_id[:, None] == my_slots[None, :], 1, 0), axis=0)
    held = held.astype(jnp.int32)

    def exchange(x):
        return lax.all_to_all(x, BOTH, split_axis=0, concat_axis=0, tiled=True)

    packed = pack(slots * shard_count, piece, slot_of_row, mine, theirs)
    packed, right_later = lax.optimization_barrier((packed, right_root))
    right_oth = lax.ppermute(
        lax.dynamic_slice_in_dim(right_later, 1 - me, 1, 0), "rep", SWAP
    )
    right_oth = fetch(right_oth)
    grad = exchange(packed).reshape(slots, block, strip)
    update, grad = apply_roots(rep, grad, left_root, right_root, right_oth)
    update, grad = lax.optimization_barrier((update, grad))
    back = exchange(update.reshape(packed.shape))
    grad_other = lax.ppermute(grad, "rep", SWAP)
    gram_left, gram_right = grams(rep, held, grad, grad_other)
    holder_id, gram_left = lax.optimization_barrier((holder_id, gram_left))
    return place_rows(rows, holder_id, offsets, back), gram_left, gram_right


def solution(mesh):
    in_specs = (P("rep", "shard", None), P(), P(), P("shard", None, None), P("shard", None, "rep"))
    out_specs = (P("shard", "rep"), P("shard", "rep", None), P("shard", "rep", None))
    return jax.shard_map(local, mesh=mesh, in_specs=in_specs, out_specs=out_specs, check_vma=False)
```
